32 devices in a mesh: depth: 4 (over y, x), panel: 8 (over z, core).
Axes of the slice: x: 2, y: 2, z: 4, core: 2. Of those that a mesh axis runs over, the one named last changes fastest.
Arguments:
- diag_blocks: float32 [4, 1024, 1024], P('depth', 'panel'), as said below
- coupling: float32 [4, 1024, 1024], P('depth', 'panel'), may hold values from -0.078125 to 0.078125
- sources: float32 [4, 1024, 256], P('depth', 'panel'), may hold values from -6 to 6
- requests: int32 [4, 128], P('depth', 'panel'), may hold values from 0 to 1023, as said below
Outputs:
- panels: float32 [4, 1024, 256], P('depth', 'panel')
- picked: float32 [4, 128, 256], P('depth', 'panel')
The draws below stay inside these ranges and needn't reach their ends.
Inputs may be any that keep to these rules, and one draw needn't show every extreme that they name: `requests`: row numbers within their block; both 0 and 1023 occur. `diag_blocks`: every diagonal block is exactly symmetric with a positive diagonal.
All inputs are finite; a program needn't handle non-finite values.
Results may differ from the reference program's by a relative error of at most 0.0001.
Values sent between devices are 32-bit elements; how exact they have to be, the bound alone decides.
A program may use at most 64 MiB of HBM per device.

```python
import math
import jax
import jax.numpy as jnp
from jax import lax

B = 1024
Q = 256
R = 128
ITERS = 2
NB = 4


def draw_diag_blocks(key, part):
    key_off, key_diag = jax.random.split(key)
    raw_values = jax.random.normal(key_off, (NB, B, B), jnp.float32)
    symmetric = (raw_values + jnp.swapaxes(raw_values, 1, 2)) * (0.5 / math.sqrt(2.0 * B))
    diag_values = jax.random.uniform(key_diag, (NB, B), jnp.float32, 3.0, 5.0)
    identity = jnp.eye(B, dtype=jnp.float32)
    return symmetric * (1.0 - identity) + diag_values[:, :, None] * identity


def draw_requests(key, part):
    row_numbers = jax.random.randint(key, (NB, R), 0, B, jnp.int32)
    return row_numbers.at[0, 0].set(B - 1).at[NB - 1, R - 1].set(0)


def level_of(own_key, shape, pieces, least, largest):
    factor_of = 1.0
    for dim, blocks in pieces:
        draws = jax.random.uniform(jax.random.fold_in(jax.random.fold_in(own_key, 6), dim), (blocks,), jnp.float32, least / len(pieces), largest / len(pieces))
        factor_of = factor_of * jnp.repeat(jnp.exp(draws), shape[dim] // blocks).reshape((-1,) + (1,) * (len(shape) - 1 - dim))
    return factor_of


def centred(key, shape, deviation, most, shards=(), kind=jnp.bfloat16):
    drawn = deviation * jax.random.normal(key, shape, jnp.float32)
    if shards:
        drawn = drawn * level_of(key, shape, shards, -0.22, 0.18)
    return jnp.clip(drawn, -most, most).astype(kind)


def setup_inputs(seed: int = 0) -> dict:
    streams_of = jax.random.split(jax.random.key(seed), 5)
    diag_blocks = draw_diag_blocks(jax.random.fold_in(streams_of[4], 71), 0)
    coupling = centred(streams_of[1], (NB, B, B), (5 * B) ** -0.5, 0.078125, ((0, 4), (1, 8)), jnp.float32)
    sources = centred(streams_of[2], (NB, B, Q), 1.0, 6.0, ((0, 4), (1, 8)), jnp.float32)
    requests = draw_requests(jax.random.fold_in(streams_of[4], 71), 0)
    return dict(diag_blocks=diag_blocks, coupling=coupling, sources=sources, requests=requests)


def jacobi(matrix, right_hand):
    diag_part = jnp.diagonal(matrix)[:, None]
    iterate = right_hand / diag_part
    for sweep_no in range(ITERS):
        image = jnp.dot(matrix, iterate, precision=lax.Precision.HIGHEST, preferred_element_type=jnp.float32)
        iterate = iterate + (right_hand - image) / diag_part
    return iterate


def reference(diag_blocks, coupling, sources, requests):
    block_total = diag_blocks.shape[0]
    left_terms = []
    carried = jnp.zeros(sources.shape[1:], jnp.float32)
    for block_no in range(block_total):
        left_terms.append(carried)
        forward = jacobi(diag_blocks[block_no], sources[block_no] - carried)
        carried = jnp.dot(coupling[block_no].T, forward, precision=lax.Precision.HIGHEST, preferred_element_type=jnp.float32)
    results = [None] * block_total
    ahead = jnp.zeros(sources.shape[1:], jnp.float32)
    for block_no in reversed(range(block_total)):
        right_term = jnp.dot(coupling[block_no], ahead, precision=lax.Precision.HIGHEST, preferred_element_type=jnp.float32)
        ahead = jacobi(diag_blocks[block_no], sources[block_no] - left_terms[block_no] - right_term)
        results[block_no] = ahead
    panels = jnp.stack(results)
    where_rows = jnp.broadcast_to(requests[:, :, None], (requests.shape[0], requests.shape[1], panels.shape[2]))
    picked = jnp.take_along_axis(panels, where_rows, axis=1)
    return (panels, picked)
```

```python
import jax
import jax.numpy as jnp
from jax import lax
from jax.experimental import pallas as pl
from jax.experimental.pallas import tpu as pltpu
from jax.sharding import PartitionSpec as P

ITERS = 2


highest = lax.Precision.HIGHEST


def passed_along(block, axis, distance):
    devices = range(lax.axis_size(axis))
    route = [(i - distance, i) for i in devices if i - distance in devices]
    return lax.ppermute(block, axis, route)


def product_rows(matrix, panel_rows):
    initial = jnp.zeros((matrix.shape[0], panel_rows.shape[1]), jnp.float32)
    shard_rows = lax.all_gather(panel_rows, "panel", axis=0, tiled=True)
    columns = lax.slice_in_dim(matrix, 0, shard_rows.shape[0], axis=1)
    return initial + jnp.dot(
        columns, shard_rows, precision=highest, preferred_element_type=jnp.float32
    )


def product_transposed(matrix, panel_rows):
    return lax.psum_scatter(
        lax.dot_general(
            matrix,
            panel_rows,
            (((0,), (0,)), ((), ())),
            precision=highest,
            preferred_element_type=jnp.float32,
        ),
        "panel",
        scatter_dimension=0,
        tiled=True,
    )


def jacobi(matrix, diag_part, right_hand):
    scaled = diag_part[:, None]
    iterate = right_hand / scaled
    for sweep_no in range(ITERS):
        image = product_rows(matrix, iterate)
        iterate = iterate + (right_hand - image) / scaled
    return iterate


def per_device_general(diag_blocks, coupling, sources, requests):
    depth_count = lax.axis_size("depth")
    depth_pos = lax.axis_index("depth")
    panel_pos = lax.axis_index("panel")
    block_count = diag_blocks.shape[0]
    row_count = diag_blocks.shape[1]
    local_cols = sources.shape[2]
    own_square = lax.dynamic_slice_in_dim(diag_blocks, panel_pos * row_count, row_count, 2)
    diag_part = jnp.diagonal(own_square, axis1=1, axis2=2)
    col_groups = max(1, local_cols // 128)
    col_width = local_cols // col_groups
    section_total = depth_count + col_groups - 1
    left_terms = jnp.zeros_like(sources)
    carried = jnp.zeros((row_count, col_width), jnp.float32)
    for section_no in range(section_total):
        column_pos = section_no - depth_pos
        active = (column_pos >= 0) & (column_pos < col_groups)
        col_start = jnp.clip(column_pos, 0, col_groups - 1) * col_width
        block_no = 0
        source_cols = lax.dynamic_slice_in_dim(sources[block_no], col_start, col_width, 1)
        stored = lax.dynamic_update_slice_in_dim(left_terms[block_no], carried, col_start, 1)
        left_terms = left_terms.at[block_no].set(jnp.where(active, stored, left_terms[block_no]))
        forward = jacobi(diag_blocks[block_no], diag_part[block_no], source_cols - carried)
        carried = product_transposed(coupling[block_no], forward)
        carried = passed_along(carried, "depth", 1)
    panels = jnp.zeros_like(sources)
    ahead = jnp.zeros((row_count, col_width), jnp.float32)
    for section_no in range(section_total):
        column_pos = section_no - (depth_count - 1 - depth_pos)
        active = (column_pos >= 0) & (column_pos < col_groups)
        col_start = jnp.clip(column_pos, 0, col_groups - 1) * col_width
        for block_no in reversed(range(block_count)):
            source_cols = lax.dynamic_slice_in_dim(sources[block_no], col_start, col_width, 1)
            left_cols = lax.dynamic_slice_in_dim(left_terms[block_no], col_start, col_width, 1)
            right_term = product_rows(coupling[block_no], ahead)
            ahead = jacobi(
                diag_blocks[block_no], diag_part[block_no], source_cols - left_cols - right_term
            )
            stored = lax.dynamic_update_slice_in_dim(panels[block_no], ahead, col_start, 1)
            panels = panels.at[block_no].set(jnp.where(active, stored, panels[block_no]))
        ahead = passed_along(ahead, "depth", -1)
    picked_rows = requests.shape[1]
    shard_rows = lax.all_gather(panels, "panel", axis=1, tiled=True)
    shard_len = shard_rows.shape[1]
    inside = (requests >= 0) & (requests < shard_len)
    clipped = jnp.clip(requests, 0, shard_len - 1)
    where_rows = jnp.broadcast_to(
        clipped[:, :, None], (block_count, picked_rows, shard_rows.shape[2])
    )
    taken = jnp.take_along_axis(shard_rows, where_rows, axis=1)
    picked = jnp.where(inside[:, :, None], taken, 0.0)
    return (panels, picked)


MESH = pl.DeviceIdType.MESH
LEFT, RIGHT, SIBLING = 0, 1, 2


def received(x, a, b, chips):
    if a == x or b == x:
        return False
    if a == b:
        return True
    if a > x and b > x:
        return a < b
    if a < x and b < x:
        return a > b
    return (a < x) == (x < chips // 2)


def split(value):
    high = value.astype(jnp.bfloat16)
    low = (value - high.astype(jnp.float32)).astype(jnp.bfloat16)
    return high, low


def sweep_kernel(
    diag_ref, coup_ref, src_ref, req_ref,
    out_ref, pick_ref,
    diag_all, coup_all, diag_hi, diag_lo, coup_hi, coup_lo,
    src_out, src_in, req_in, rhs, iterate, image, stacked, scale,
    left_in, ahead_in, link_out, res_out, res_in, pick_out, pick_in, pick_rows,
    d_send, d_recv, c_send, c_recv, s_send, s_recv, q_send, q_recv,
    chain_send, chain_recv, r_send, r_recv, p_send, p_recv,
):
    depth_count = lax.axis_size("depth")
    count = lax.axis_size("panel")
    depth = lax.axis_index("depth")
    me = lax.axis_index("panel")
    chips = count // 2
    chip = me // 2
    core = lax.rem(me, 2)
    rows = diag_ref.shape[0]
    order = diag_ref.shape[1]
    cols = src_out.shape[1]
    width = order // chips
    last = depth_count - 1

    barrier = pltpu.get_barrier_semaphore()
    for off in range(1, count):
        pl.semaphore_signal(
            barrier, inc=1, device_id={"panel": lax.rem(me + off, count)}, device_id_type=MESH
        )

    @pl.when(depth > 0)
    def _():
        pl.semaphore_signal(barrier, inc=1, device_id={"depth": depth - 1}, device_id_type=MESH)

    @pl.when(depth < last)
    def _():
        pl.semaphore_signal(barrier, inc=1, device_id={"depth": depth + 1}, device_id_type=MESH)

    src_out[...] = src_ref[...].T.reshape(count, cols, rows)
    diag_all[me] = diag_ref[...]
    coup_all[me] = coup_ref[...]

    ends = (depth == 0).astype(jnp.int32) + (depth == last).astype(jnp.int32)
    pl.semaphore_wait(barrier, count + 1 - ends)

    neighbour = {LEFT: me - 2, RIGHT: me + 2, SIBLING: me + 1 - 2 * core}

    def diag_copy(way, a, b, of_core):
        slab = 2 * a + of_core
        part = diag_all.at[slab, :, pl.ds(b * width, width)]
        return pltpu.make_async_remote_copy(
            src_ref=part, dst_ref=part,
            send_sem=d_send.at[way, a, b], recv_sem=d_recv.at[slab, b],
            device_id={"panel": neighbour[way]}, device_id_type=MESH,
        )

    def coup_copy(way, a, of_core):
        slab = 2 * a + of_core
        part = coup_all.at[slab]
        return pltpu.make_async_remote_copy(
            src_ref=part, dst_ref=part,
            send_sem=c_send.at[way, a], recv_sem=c_recv.at[slab],
            device_id={"panel": neighbour[way]}, device_id_type=MESH,
        )

    def diag_ways(x, a, b):
        ways = []
        if a >= x and any(received(y, a, b, chips) for y in range(x)):
            ways.append(LEFT)
        if a <= x and any(received(y, a, b, chips) for y in range(x + 1, chips)):
            ways.append(RIGHT)
        if a == x or received(x, a, b, chips):
            ways.append(SIBLING)
        return ways

    def coup_ways(x, a):
        ways = []
        if a >= x and x > 0:
            ways.append(LEFT)
        if a <= x and x < chips - 1:
            ways.append(RIGHT)
        ways.append(SIBLING)
        return ways

    def arrivals(x):
        for dist in range(1, chips):
            for a in (x - dist, x + dist):
                if 0 <= a < chips:
                    yield a

    def own_first(x, a):
        return sorted(range(chips), key=lambda b: abs(b - a))

    def src_copy(off):
        to = lax.rem(me + off, count)
        return pltpu.make_async_remote_copy(
            src_ref=src_out.at[to], dst_ref=src_in.at[me],
            send_sem=s_send.at[off], recv_sem=s_recv.at[off],
            device_id={"panel": to}, device_id_type=MESH,
        )

    def req_copy(off):
        return pltpu.make_async_remote_copy(
            src_ref=req_ref, dst_ref=req_in.at[me],
            send_sem=q_send.at[off], recv_sem=q_recv.at[off],
            device_id={"panel": lax.rem(me + off, count)}, device_id_type=MESH,
        )

    for off in range(1, count):
        src_copy(off).start()
        req_copy(off).start()
    src_in[me] = src_out[me]
    req_in[me] = req_ref[...]

    for x in range(chips):
        @pl.when(chip == x)
        def _():
            for b in own_first(x, x):
                for way in diag_ways(x, x, b):
                    diag_copy(way, x, b, core).start()
            for a in arrivals(x):
                for b in own_first(x, a):
                    if received(x, a, b, chips):
                        diag_copy(SIBLING, a, b, core).wait_recv()
                        for way in diag_ways(x, a, b):
                            diag_copy(way, a, b, core).start()
            for way in coup_ways(x, x):
                coup_copy(way, x, core).start()
            for a in range(chips):
                for b in range(chips):
                    if a == x or received(x, a, b, chips):
                        diag_copy(SIBLING, a, b, 1 - core).wait_recv()

    for off in range(1, count):
        src_copy(off).wait_recv()
        req_copy(off).wait_recv()

    def expand(at, carry):
        a, b = at // chips, lax.rem(at, chips)
        straddle = (a < chip) != (b < chip)
        from_left = chip < chips // 2
        both_right = (a > chip) & (b > chip)
        got = (a == chip) | (
            (b != chip)
            & (
                (a == b)
                | (both_right & (a < b))
                | ((a < chip) & (b < chip) & (a > b))
                | (straddle & ((a < chip) == from_left))
            )
        )
        rows_at = pl.ds(pl.multiple_of(a * width, width), width)
        cols_at = pl.ds(pl.multiple_of(b * width, width), width)

        @pl.when(got)
        def _():
            high, low = split(diag_all[pl.ds(2 * a, 2), :, cols_at].reshape(width, width))
            diag_hi[rows_at, cols_at] = high
            diag_lo[rows_at, cols_at] = low

        @pl.when(jnp.logical_not(got))
        def _():
            high, low = split(diag_all[pl.ds(2 * b, 2), :, rows_at].reshape(width, width).T)
            diag_hi[rows_at, cols_at] = high
            diag_lo[rows_at, cols_at] = low

        return carry

    lax.fori_loop(0, chips * chips, expand, 0)

    eye = lax.broadcasted_iota(jnp.int32, (rows, rows), 0) == lax.broadcasted_iota(
        jnp.int32, (rows, rows), 1
    )
    for p in range(count):
        lanes = slice(p * rows, (p + 1) * rows)
        scale[:, lanes] = jnp.sum(
            jnp.where(eye, diag_all[p, :, lanes], 0.0), axis=0, keepdims=True
        )
        rhs[:, lanes] = src_in[p]

    def widen_coup(slab):
        high, low = split(coup_all[slab])
        at = pl.ds(pl.multiple_of(slab * rows, rows), rows)
        coup_hi[at, :] = high
        coup_lo[at, :] = low

    tile = width

    def product(value, high_ref, low_ref, contract):
        high, low = split(value)
        stacked[0:cols] = high
        stacked[cols : 2 * cols] = low

        def one(n, carry):
            at = pl.ds(pl.multiple_of(n * tile, tile), tile)
            pick = (slice(None), at) if contract == 0 else (at, slice(None))
            dims = (((1,), (contract,)), ((), ()))
            both = lax.dot_general(
                stacked[...], high_ref[pick], dims, preferred_element_type=jnp.float32
            )
            small = lax.dot_general(
                stacked[0:cols], low_ref[pick], dims, preferred_element_type=jnp.float32
            )
            image[:, at] = both[0:cols] + (both[cols : 2 * cols] + small)
            return carry

        lax.fori_loop(0, order // tile, one, 0)

    def jacobi_columns():
        iterate[...] = rhs[...] / scale[...]

        def step(sweep_no, carry):
            product(iterate[...], diag_hi, diag_lo, 0)
            iterate[...] = iterate[...] + (rhs[...] - image[...]) / scale[...]
            return carry

        lax.fori_loop(0, ITERS, step, 0)

    @pl.when(depth == 0)
    def _():
        jacobi_columns()

    for x in range(chips):
        @pl.when(chip == x)
        def _():
            widen_coup(2 * x + core)
            for a in arrivals(x):
                coup_copy(SIBLING, a, core).wait_recv()
                for way in coup_ways(x, a):
                    coup_copy(way, a, core).start()
                widen_coup(2 * a + core)
    for a in range(chips):
        coup_copy(SIBLING, a, 1 - core).wait_recv()
        widen_coup(2 * a + 1 - core)

    def chain_copy(way, to):
        return pltpu.make_async_remote_copy(
            src_ref=link_out.at[way], dst_ref=left_in if way == 0 else ahead_in,
            send_sem=chain_send.at[way], recv_sem=chain_recv.at[way],
            device_id={"depth": to}, device_id_type=MESH,
        )

    @pl.when(depth > 0)
    def _():
        chain_copy(0, depth).wait_recv()
        rhs[...] = rhs[...] - left_in[...]

    @pl.when((depth > 0) & (depth < last))
    def _():
        jacobi_columns()

    @pl.when(depth < last)
    def _():
        product(iterate[...], coup_hi, coup_lo, 0)
        link_out[0] = image[...]
        chain_copy(0, depth + 1).start()
        chain_copy(1, depth).wait_recv()
        product(ahead_in[...], coup_hi, coup_lo, 1)
        rhs[...] = rhs[...] - image[...]

    jacobi_columns()

    @pl.when(depth > 0)
    def _():
        link_out[1] = iterate[...]
        chain_copy(1, depth - 1).start()

    def res_copy(off):
        to = lax.rem(me + off, count)
        return pltpu.make_async_remote_copy(
            src_ref=res_out.at[to], dst_ref=res_in.at[me],
            send_sem=r_send.at[off], recv_sem=r_recv.at[off],
            device_id={"panel": to}, device_id_type=MESH,
        )

    def pick_copy(off):
        return pltpu.make_async_remote_copy(
            src_ref=pick_out, dst_ref=pick_in.at[me],
            send_sem=p_send.at[off], recv_sem=p_recv.at[off],
            device_id={"panel": lax.rem(me + off, count)}, device_id_type=MESH,
        )

    for p in range(count):
        res_out[p] = iterate[:, p * rows : (p + 1) * rows]
    for off in range(1, count):
        res_copy(off).start()
    value = iterate[...]
    high, low = split(value)
    rest = ((value - high.astype(jnp.float32)) - low.astype(jnp.float32)).astype(jnp.bfloat16)
    wanted = jnp.sum(req_in[...], axis=0)[0:1]
    chosen = lax.broadcasted_iota(jnp.int32, (order, wanted.shape[1]), 0) == wanted
    chosen = chosen.astype(jnp.float32).astype(jnp.bfloat16)

    def take(term):
        return jnp.dot(term, chosen, preferred_element_type=jnp.float32)

    pick_out[...] = (take(rest) + take(low)) + take(high)
    for off in range(1, count):
        pick_copy(off).start()
    res_in[me] = res_out[me]
    pick_in[me] = pick_out[...]
    for off in range(1, count):
        res_copy(off).wait_recv()
    out_ref[...] = res_in[...].reshape(count * cols, rows).T
    for off in range(1, count):
        pick_copy(off).wait_recv()
    pick_rows[...] = pick_in[...].reshape(count * cols, pick_out.shape[1]).T
    mine = pick_ref.shape[0]
    pick_ref[...] = pick_rows[pl.ds(pl.multiple_of(me * mine, mine), mine), :]

    for off in range(1, count):
        src_copy(off).wait_send()
        req_copy(off).wait_send()
        res_copy(off).wait_send()
        pick_copy(off).wait_send()

    @pl.when(depth < last)
    def _():
        chain_copy(0, depth + 1).wait_send()

    @pl.when(depth > 0)
    def _():
        chain_copy(1, depth - 1).wait_send()

    for x in range(chips):
        @pl.when(chip == x)
        def _():
            for a in range(chips):
                for b in range(chips):
                    for way in diag_ways(x, a, b):
                        diag_copy(way, a, b, core).wait_send()
                for way in coup_ways(x, a):
                    coup_copy(way, a, core).wait_send()


def per_device(diag_blocks, coupling, sources, requests):
    count = lax.axis_size("panel")
    block_count, rows, order = diag_blocks.shape
    total = sources.shape[2]
    mine = requests.shape[1]
    if (
        block_count != 1
        or count % 2
        or rows % 128
        or order != rows * count
        or total % (16 * count)
        or mine % 8
        or (mine * count) % 128
    ):
        return per_device_general(diag_blocks, coupling, sources, requests)
    cols = total // count
    chips = count // 2
    spots = jnp.zeros((1, mine * count), jnp.int32)
    spots = lax.dynamic_update_slice(spots, requests, (0, lax.axis_index("panel") * mine))
    spots = jnp.broadcast_to(spots, (8, mine * count))
    f32, half = jnp.float32, jnp.bfloat16
    vmem = pltpu.VMEM
    dma = pltpu.SemaphoreType.DMA
    panels, picked = pl.pallas_call(
        sweep_kernel,
        out_shape=(
            jax.ShapeDtypeStruct((rows, total), f32),
            jax.ShapeDtypeStruct((mine, total), f32),
        ),
        in_specs=[pl.BlockSpec(memory_space=vmem)] * 4,
        out_specs=(pl.BlockSpec(memory_space=vmem), pl.BlockSpec(memory_space=vmem)),
        scratch_shapes=[
            vmem((count, rows, order), f32),
            vmem((count, rows, order), f32),
            vmem((order, order), half),
            vmem((order, order), half),
            vmem((order, order), half),
            vmem((order, order), half),
            vmem((count, cols, rows), f32),
            vmem((count, cols, rows), f32),
            vmem((count, 8, mine * count), jnp.int32),
            vmem((cols, order), f32),
            vmem((cols, order), f32),
            vmem((cols, order), f32),
            vmem((2 * cols, order), half),
            vmem((1, order), f32),
            vmem((cols, order), f32),
            vmem((cols, order), f32),
            vmem((2, cols, order), f32),
            vmem((count, cols, rows), f32),
            vmem((count, cols, rows), f32),
            vmem((cols, mine * count), f32),
            vmem((count, cols, mine * count), f32),
            vmem((mine * count, total), f32),
            dma((3, chips, chips)),
            dma((count, chips)),
            dma((3, chips)),
            dma((count,)),
            dma((count,)),
            dma((count,)),
            dma((count,)),
            dma((count,)),
            dma((2,)),
            dma((2,)),
            dma((count,)),
            dma((count,)),
            dma((count,)),
            dma((count,)),
        ],
        compiler_params=pltpu.CompilerParams(
            collective_id=0, has_side_effects=True, vmem_limit_bytes=48 * 2**20
        ),
        cost_estimate=pl.CostEstimate(
            flops=36 * order * order * cols, bytes_accessed=16 * rows * order, transcendentals=0
        ),
    )(diag_blocks[0], coupling[0], sources[0], spots)
    return panels[None], picked[None]


def solution(mesh):
    placed = (
        P("depth", "panel", None),
        P("depth", "panel", None),
        P("depth", "panel", None),
        P("depth", "panel"),
    )
    return jax.shard_map(
        per_device,
        mesh=mesh,
        in_specs=placed,
        out_specs=(P("depth", "panel", None), P("depth", "panel", None)),
        check_vma=False,
    )
```

```python
import jax
import jax.numpy as jnp
from jax import lax
from jax.experimental import pallas as pl
from jax.experimental.pallas import tpu as pltpu
from jax.sharding import PartitionSpec as P

ITERS = 2


highest = lax.Precision.HIGHEST


def passed_along(block, axis, distance):
    devices = range(lax.axis_size(axis))
    route = [(i - distance, i) for i in devices if i - distance in devices]
    return lax.ppermute(block, axis, route)


def product_rows(matrix, panel_rows):
    initial = jnp.zeros((matrix.shape[0], panel_rows.shape[1]), jnp.float32)
    shard_rows = lax.all_gather(panel_rows, "panel", axis=0, tiled=True)
    columns = lax.slice_in_dim(matrix, 0, shard_rows.shape[0], axis=1)
    return initial + jnp.dot(
        columns, shard_rows, precision=highest, preferred_element_type=jnp.float32
    )


def product_transposed(matrix, panel_rows):
    return lax.psum_scatter(
        lax.dot_general(
            matrix,
            panel_rows,
            (((0,), (0,)), ((), ())),
            precision=highest,
            preferred_element_type=jnp.float32,
        ),
        "panel",
        scatter_dimension=0,
        tiled=True,
    )


def jacobi(matrix, diag_part, right_hand):
    scaled = diag_part[:, None]
    iterate = right_hand / scaled
    for sweep_no in range(ITERS):
        image = product_rows(matrix, iterate)
        iterate = iterate + (right_hand - image) / scaled
    return iterate


def per_device_general(diag_blocks, coupling, sources, requests):
    depth_count = lax.axis_size("depth")
    depth_pos = lax.axis_index("depth")
    panel_pos = lax.axis_index("panel")
    block_count = diag_blocks.shape[0]
    row_count = diag_blocks.shape[1]
    local_cols = sources.shape[2]
    own_square = lax.dynamic_slice_in_dim(diag_blocks, panel_pos * row_count, row_count, 2)
    diag_part = jnp.diagonal(own_square, axis1=1, axis2=2)
    col_groups = max(1, local_cols // 128)
    col_width = local_cols // col_groups
    section_total = depth_count + col_groups - 1
    left_terms = jnp.zeros_like(sources)
    carried = jnp.zeros((row_count, col_width), jnp.float32)
    for section_no in range(section_total):
        column_pos = section_no - depth_pos
        active = (column_pos >= 0) & (column_pos < col_groups)
        col_start = jnp.clip(column_pos, 0, col_groups - 1) * col_width
        block_no = 0
        source_cols = lax.dynamic_slice_in_dim(sources[block_no], col_start, col_width, 1)
        stored = lax.dynamic_update_slice_in_dim(left_terms[block_no], carried, col_start, 1)
        left_terms = left_terms.at[block_no].set(jnp.where(active, stored, left_terms[block_no]))
        forward = jacobi(diag_blocks[block_no], diag_part[block_no], source_cols - carried)
        carried = product_transposed(coupling[block_no], forward)
        carried = passed_along(carried, "depth", 1)
    panels = jnp.zeros_like(sources)
    ahead = jnp.zeros((row_count, col_width), jnp.float32)
    for section_no in range(section_total):
        column_pos = section_no - (depth_count - 1 - depth_pos)
        active = (column_pos >= 0) & (column_pos < col_groups)
        col_start = jnp.clip(column_pos, 0, col_groups - 1) * col_width
        for block_no in reversed(range(block_count)):
            source_cols = lax.dynamic_slice_in_dim(sources[block_no], col_start, col_width, 1)
            left_cols = lax.dynamic_slice_in_dim(left_terms[block_no], col_start, col_width, 1)
            right_term = product_rows(coupling[block_no], ahead)
            ahead = jacobi(
                diag_blocks[block_no], diag_part[block_no], source_cols - left_cols - right_term
            )
            stored = lax.dynamic_update_slice_in_dim(panels[block_no], ahead, col_start, 1)
            panels = panels.at[block_no].set(jnp.where(active, stored, panels[block_no]))
        ahead = passed_along(ahead, "depth", -1)
    picked_rows = requests.shape[1]
    shard_rows = lax.all_gather(panels, "panel", axis=1, tiled=True)
    shard_len = shard_rows.shape[1]
    inside = (requests >= 0) & (requests < shard_len)
    clipped = jnp.clip(requests, 0, shard_len - 1)
    where_rows = jnp.broadcast_to(
        clipped[:, :, None], (block_count, picked_rows, shard_rows.shape[2])
    )
    taken = jnp.take_along_axis(shard_rows, where_rows, axis=1)
    picked = jnp.where(inside[:, :, None], taken, 0.0)
    return (panels, picked)


MESH = pl.DeviceIdType.MESH
LEFT, RIGHT, SIBLING = 0, 1, 2


def received(x, a, b, chips):
    if a == x or b == x:
        return False
    if a == b:
        return True
    if a > x and b > x:
        return a < b
    if a < x and b < x:
        return a > b
    return (a < x) == (x < chips // 2)


def split(value):
    high = value.astype(jnp.bfloat16)
    low = (value - high.astype(jnp.float32)).astype(jnp.bfloat16)
    return high, low


def sweep_kernel(
    diag_ref, coup_ref, src_ref, req_ref,
    out_ref, pick_ref,
    diag_all, coup_all, diag_hi, diag_lo, map_hi, map_lo, edge_hi, edge_lo, part_hi, part_lo, edge,
    src_out, src_in, req_in, rhs, iterate, forward, stacked, scale, scale_col, factors,
    left_in, ahead_in, link_out, res_out, res_in, pick_out, pick_in, pick_rows,
    d_send, d_recv, c_send, c_recv, s_send, s_recv, q_send, q_recv,
    chain_send, chain_recv, r_send, r_recv, p_send, p_recv,
):
    depth_count = lax.axis_size("depth")
    count = lax.axis_size("panel")
    depth = lax.axis_index("depth")
    me = lax.axis_index("panel")
    chips = count // 2
    chip = me // 2
    core = lax.rem(me, 2)
    rows = diag_ref.shape[0]
    order = diag_ref.shape[1]
    cols = src_out.shape[1]
    width = order // chips
    last = depth_count - 1

    barrier = pltpu.get_barrier_semaphore()
    for off in range(1, count):
        pl.semaphore_signal(
            barrier, inc=1, device_id={"panel": lax.rem(me + off, count)}, device_id_type=MESH
        )

    @pl.when(depth > 0)
    def _():
        pl.semaphore_signal(barrier, inc=1, device_id={"depth": depth - 1}, device_id_type=MESH)

    @pl.when(depth < last)
    def _():
        pl.semaphore_signal(barrier, inc=1, device_id={"depth": depth + 1}, device_id_type=MESH)

    src_out[...] = src_ref[...].T.reshape(count, cols, rows)
    diag_all[me] = diag_ref[...]
    coup_all[me] = coup_ref[...]

    ends = (depth == 0).astype(jnp.int32) + (depth == last).astype(jnp.int32)
    pl.semaphore_wait(barrier, count + 1 - ends)

    neighbour = {LEFT: me - 2, RIGHT: me + 2, SIBLING: me + 1 - 2 * core}

    def diag_copy(way, a, b, of_core):
        slab = 2 * a + of_core
        part = diag_all.at[slab, :, pl.ds(b * width, width)]
        return pltpu.make_async_remote_copy(
            src_ref=part, dst_ref=part,
            send_sem=d_send.at[way, a, b], recv_sem=d_recv.at[slab, b],
            device_id={"panel": neighbour[way]}, device_id_type=MESH,
        )

    def coup_copy(way, a, of_core):
        slab = 2 * a + of_core
        part = coup_all.at[slab]
        return pltpu.make_async_remote_copy(
            src_ref=part, dst_ref=part,
            send_sem=c_send.at[way, a], recv_sem=c_recv.at[slab],
            device_id={"panel": neighbour[way]}, device_id_type=MESH,
        )

    def diag_ways(x, a, b):
        ways = []
        if a >= x and any(received(y, a, b, chips) for y in range(x)):
            ways.append(LEFT)
        if a <= x and any(received(y, a, b, chips) for y in range(x + 1, chips)):
            ways.append(RIGHT)
        if a == x or received(x, a, b, chips):
            ways.append(SIBLING)
        return ways

    def arrivals(x):
        for dist in range(1, chips):
            for a in (x - dist, x + dist):
                if 0 <= a < chips:
                    yield a

    def own_first(x, a):
        return sorted(range(chips), key=lambda b: abs(b - a))

    def src_copy(off):
        to = lax.rem(me + off, count)
        return pltpu.make_async_remote_copy(
            src_ref=src_out.at[to], dst_ref=src_in.at[me],
            send_sem=s_send.at[off], recv_sem=s_recv.at[off],
            device_id={"panel": to}, device_id_type=MESH,
        )

    def req_copy(off):
        return pltpu.make_async_remote_copy(
            src_ref=req_ref, dst_ref=req_in.at[me],
            send_sem=q_send.at[off], recv_sem=q_recv.at[off],
            device_id={"panel": lax.rem(me + off, count)}, device_id_type=MESH,
        )

    for off in range(1, count):
        src_copy(off).start()
        req_copy(off).start()
    src_in[me] = src_out[me]
    req_in[me] = req_ref[...]

    for x in range(chips):
        @pl.when(chip == x)
        def _():
            for b in own_first(x, x):
                for way in diag_ways(x, x, b):
                    diag_copy(way, x, b, core).start()
            for a in arrivals(x):
                for b in own_first(x, a):
                    if received(x, a, b, chips):
                        diag_copy(SIBLING, a, b, core).wait_recv()
                        for way in diag_ways(x, a, b):
                            diag_copy(way, a, b, core).start()
            for a in range(chips):
                for b in range(chips):
                    if a == x or received(x, a, b, chips):
                        diag_copy(SIBLING, a, b, 1 - core).wait_recv()

    def coup_each(a, act):
        @pl.when((a >= chip) & (chip > 0))
        def _():
            act(coup_copy(LEFT, a, core))

        @pl.when((a <= chip) & (chip < chips - 1))
        def _():
            act(coup_copy(RIGHT, a, core))

        act(coup_copy(SIBLING, a, core))

    @pl.when(depth < last)
    def _():
        coup_each(chip, lambda copy: copy.start())

    for off in range(1, count):
        src_copy(off).wait_recv()
        req_copy(off).wait_recv()

    def expand(at, carry):
        a, b = at // chips, lax.rem(at, chips)
        straddle = (a < chip) != (b < chip)
        from_left = chip < chips // 2
        both_right = (a > chip) & (b > chip)
        got = (a == chip) | (
            (b != chip)
            & (
                (a == b)
                | (both_right & (a < b))
                | ((a < chip) & (b < chip) & (a > b))
                | (straddle & ((a < chip) == from_left))
            )
        )
        rows_at = pl.ds(pl.multiple_of(a * width, width), width)
        cols_at = pl.ds(pl.multiple_of(b * width, width), width)

        @pl.when(got)
        def _():
            high, low = split(diag_all[pl.ds(2 * a, 2), :, cols_at].reshape(width, width))
            diag_hi[rows_at, cols_at] = high
            diag_lo[rows_at, cols_at] = low

        @pl.when(jnp.logical_not(got))
        def _():
            high, low = split(diag_all[pl.ds(2 * b, 2), :, rows_at].reshape(width, width).T)
            diag_hi[rows_at, cols_at] = high
            diag_lo[rows_at, cols_at] = low

        return carry

    lax.fori_loop(0, chips * chips, expand, 0)

    eye = lax.broadcasted_iota(jnp.int32, (rows, rows), 0) == lax.broadcasted_iota(
        jnp.int32, (rows, rows), 1
    )
    for p in range(count):
        lanes = slice(p * rows, (p + 1) * rows)
        scale[:, lanes] = jnp.sum(
            jnp.where(eye, diag_all[p, :, lanes], 0.0), axis=0, keepdims=True
        )
        scale_col[lanes, :] = jnp.sum(
            jnp.where(eye, diag_all[p, :, lanes], 0.0), axis=1, keepdims=True
        )
        rhs[:, lanes] = src_in[p]

    tile = width
    tall = 2 * width
    tiny = 1.0 / order

    def sums(n, carry):
        at = pl.ds(pl.multiple_of(n * tile, tile), tile)
        total = jnp.sum(jnp.abs(diag_hi[:, at].astype(jnp.float32)) * tiny, axis=0, keepdims=True)
        return jnp.maximum(carry, total / scale[:, at])

    largest = lax.fori_loop(0, chips, sums, jnp.zeros((1, tile), jnp.float32))
    largest = jnp.max(largest, axis=1, keepdims=True) * (1.02 * order)
    largest = jnp.maximum(largest, 1.0)
    least = jnp.min(scale[...], axis=1, keepdims=True)
    factors[0:1] = jnp.broadcast_to(largest, (1, tile))
    factors[1:2] = jnp.broadcast_to(least, (1, tile))

    def identity(i, n):
        down = lax.broadcasted_iota(jnp.int32, (tile, tile), 0) + i * tile
        over = lax.broadcasted_iota(jnp.int32, (tile, tile), 1) + n * tile
        return down == over

    def over_diag(value, rows_at):
        part = scale_col[rows_at, :]
        ease = jnp.where(part > 1.0, 2.0**-30, 1.0)
        return (value * ease) * (1.0 / (part * ease))

    def across(at):
        return factors[1:2] / scale[:, at] / factors[0:1] / factors[0:1]

    def first_step(at_tile, carry):
        i, n = at_tile // chips, lax.rem(at_tile, chips)
        rows_at = pl.ds(pl.multiple_of(i * tile, tile), tile)
        at = pl.ds(pl.multiple_of(n * tile, tile), tile)
        ratio = diag_hi[rows_at, at].astype(jnp.float32) + diag_lo[rows_at, at].astype(jnp.float32)
        ratio = over_diag(ratio, rows_at)
        high, low = split((jnp.where(identity(i, n), 2.0, 0.0) - ratio) * across(at))
        edge_hi[rows_at, at] = high
        edge_lo[rows_at, at] = low
        return carry

    lax.fori_loop(0, chips * chips, first_step, 0)

    def dot(left, right, contract=0):
        return lax.dot_general(
            left, right, (((1,), (contract,)), ((), ())), preferred_element_type=jnp.float32
        )

    def second_step(at_tile, carry):
        i, n = at_tile // chips, lax.rem(at_tile, chips)
        rows_at = pl.ds(pl.multiple_of(i * tile, tile), tile)
        at = pl.ds(pl.multiple_of(n * tile, tile), tile)
        moved = dot(diag_hi[rows_at, :], edge_hi[:, at]) + (
            dot(diag_hi[rows_at, :], edge_lo[:, at]) + dot(diag_lo[rows_at, :], edge_hi[:, at])
        )
        start = edge_hi[rows_at, at].astype(jnp.float32) + edge_lo[rows_at, at].astype(jnp.float32)
        moved = jnp.where(identity(i, n), across(at), 0.0) - over_diag(moved, rows_at)
        high, low = split(start + moved)
        map_hi[rows_at, at] = high
        map_lo[rows_at, at] = low
        return carry

    lax.fori_loop(0, chips * chips, second_step, 0)

    def add_slab(a, first):
        high, low = split(coup_all[pl.ds(2 * a, 2)].reshape(width, order))
        part_hi[...] = high
        part_lo[...] = low
        along = pl.ds(pl.multiple_of(a * width, width), width)

        def one(at_tile, carry):
            i, n = lax.rem(at_tile, order // tall), at_tile // (order // tall)
            rows_at = pl.ds(pl.multiple_of(i * tall, tall), tall)
            at = pl.ds(pl.multiple_of(n * tile, tile), tile)
            term = dot(map_hi[rows_at, along], part_hi[:, at]) + (
                dot(map_hi[rows_at, along], part_lo[:, at])
                + dot(map_lo[rows_at, along], part_hi[:, at])
            )
            edge[rows_at, at] = term if first else edge[rows_at, at] + term
            return carry

        lax.fori_loop(0, (order // tall) * chips, one, 0)

    @pl.when(depth < last)
    def _():
        coup_copy(SIBLING, chip, 1 - core).wait_recv()
        add_slab(chip, True)
        for dist in range(1, chips):
            sides = [(chip - dist, chip - dist >= 0), (chip + dist, chip + dist < chips)]
            for a, there in sides:
                @pl.when(there)
                def _():
                    coup_copy(SIBLING, a, core).wait_recv()
                    coup_each(a, lambda copy: copy.start())

            for a, there in sides:
                @pl.when(there)
                def _():
                    coup_copy(SIBLING, a, 1 - core).wait_recv()
                    add_slab(a, False)

        def narrow(i, carry):
            rows_at = pl.ds(pl.multiple_of(i * tile, tile), tile)
            high, low = split(edge[rows_at, :])
            edge_hi[rows_at, :] = high
            edge_lo[rows_at, :] = low
            return carry

        lax.fori_loop(0, chips, narrow, 0)

    def product(value, high_ref, low_ref, contract, finish):
        high, low = split(value)
        stacked[0:cols] = high
        stacked[cols : 2 * cols] = low

        def one(n, carry):
            at = pl.ds(pl.multiple_of(n * tile, tile), tile)
            pick = (slice(None), at) if contract == 0 else (at, slice(None))
            both = dot(stacked[...], high_ref[pick], contract)
            small = dot(stacked[0:cols], low_ref[pick], contract)
            image = both[0:cols] + (both[cols : 2 * cols] + small)
            finish(n, at, image * factors[0:1] / factors[1:2] * factors[0:1])
            return carry

        lax.fori_loop(0, chips, one, 0)

    def chain_copy(way, n, to):
        at = pl.ds(pl.multiple_of(n * tile, tile), tile)
        into = left_in if way == 0 else ahead_in
        return pltpu.make_async_remote_copy(
            src_ref=link_out.at[way, :, at], dst_ref=into.at[:, at],
            send_sem=chain_send.at[way, n], recv_sem=chain_recv.at[way, n],
            device_id={"depth": to}, device_id_type=MESH,
        )

    def send_left(n, at, image):
        link_out[0, :, at] = image
        chain_copy(0, n, depth + 1).start()

    def keep_forward(n, at, image):
        forward[:, at] = image

    def send_panel(n, at, image):
        iterate[:, at] = image

        @pl.when(depth > 0)
        def _():
            link_out[1, :, at] = image
            chain_copy(1, n, depth - 1).start()

    @pl.when(depth > 0)
    def _():
        for n in range(chips):
            chain_copy(0, n, depth).wait_recv()
        rhs[...] = rhs[...] - left_in[...]

    @pl.when(depth < last)
    def _():
        product(rhs[...], edge_hi, edge_lo, 0, send_left)
        product(rhs[...], map_hi, map_lo, 0, keep_forward)
        for n in range(chips):
            chain_copy(1, n, depth).wait_recv()
        product(
            ahead_in[...], edge_hi, edge_lo, 1,
            lambda n, at, image: send_panel(n, at, forward[:, at] - image),
        )

    @pl.when(depth == last)
    def _():
        product(rhs[...], map_hi, map_lo, 0, send_panel)

    def res_copy(off):
        to = lax.rem(me + off, count)
        return pltpu.make_async_remote_copy(
            src_ref=res_out.at[to], dst_ref=res_in.at[me],
            send_sem=r_send.at[off], recv_sem=r_recv.at[off],
            device_id={"panel": to}, device_id_type=MESH,
        )

    def pick_copy(off):
        return pltpu.make_async_remote_copy(
            src_ref=pick_out, dst_ref=pick_in.at[me],
            send_sem=p_send.at[off], recv_sem=p_recv.at[off],
            device_id={"panel": lax.rem(me + off, count)}, device_id_type=MESH,
        )

    for p in range(count):
        res_out[p] = iterate[:, p * rows : (p + 1) * rows]
    for off in range(1, count):
        res_copy(off).start()
    value = iterate[...]
    high, low = split(value)
    rest = ((value - high.astype(jnp.float32)) - low.astype(jnp.float32)).astype(jnp.bfloat16)
    wanted = jnp.sum(req_in[...], axis=0)[0:1]
    chosen = lax.broadcasted_iota(jnp.int32, (order, wanted.shape[1]), 0) == wanted
    chosen = chosen.astype(jnp.float32).astype(jnp.bfloat16)

    def take(term):
        return jnp.dot(term, chosen, preferred_element_type=jnp.float32)

    pick_out[...] = (take(rest) + take(low)) + take(high)
    for off in range(1, count):
        pick_copy(off).start()
    res_in[me] = res_out[me]
    pick_in[me] = pick_out[...]
    for off in range(1, count):
        res_copy(off).wait_recv()
    out_ref[...] = res_in[...].reshape(count * cols, rows).T
    for off in range(1, count):
        pick_copy(off).wait_recv()
    pick_rows[...] = pick_in[...].reshape(count * cols, pick_out.shape[1]).T
    mine = pick_ref.shape[0]
    pick_ref[...] = pick_rows[pl.ds(pl.multiple_of(me * mine, mine), mine), :]

    for off in range(1, count):
        src_copy(off).wait_send()
        req_copy(off).wait_send()
        res_copy(off).wait_send()
        pick_copy(off).wait_send()

    @pl.when(depth < last)
    def _():
        for n in range(chips):
            chain_copy(0, n, depth + 1).wait_send()
        for a in range(chips):
            coup_each(a, lambda copy: copy.wait_send())

    @pl.when(depth > 0)
    def _():
        for n in range(chips):
            chain_copy(1, n, depth - 1).wait_send()

    for x in range(chips):
        @pl.when(chip == x)
        def _():
            for a in range(chips):
                for b in range(chips):
                    for way in diag_ways(x, a, b):
                        diag_copy(way, a, b, core).wait_send()


def per_device(diag_blocks, coupling, sources, requests):
    count = lax.axis_size("panel")
    block_count, rows, order = diag_blocks.shape
    total = sources.shape[2]
    mine = requests.shape[1]
    if (
        block_count != 1
        or count % 2
        or rows % 128
        or order != rows * count
        or total % (16 * count)
        or mine % 8
        or (mine * count) % 128
    ):
        return per_device_general(diag_blocks, coupling, sources, requests)
    cols = total // count
    chips = count // 2
    spots = jnp.zeros((1, mine * count), jnp.int32)
    spots = lax.dynamic_update_slice(spots, requests, (0, lax.axis_index("panel") * mine))
    spots = jnp.broadcast_to(spots, (8, mine * count))
    f32, half = jnp.float32, jnp.bfloat16
    vmem = pltpu.VMEM
    dma = pltpu.SemaphoreType.DMA
    panels, picked = pl.pallas_call(
        sweep_kernel,
        out_shape=(
            jax.ShapeDtypeStruct((rows, total), f32),
            jax.ShapeDtypeStruct((mine, total), f32),
        ),
        in_specs=[pl.BlockSpec(memory_space=vmem)] * 4,
        out_specs=(pl.BlockSpec(memory_space=vmem), pl.BlockSpec(memory_space=vmem)),
        scratch_shapes=[
            vmem((count, rows, order), f32),
            vmem((count, rows, order), f32),
            vmem((order, order), half),
            vmem((order, order), half),
            vmem((order, order), half),
            vmem((order, order), half),
            vmem((order, order), half),
            vmem((order, order), half),
            vmem((2 * rows, order), half),
            vmem((2 * rows, order), half),
            vmem((order, order), f32),
            vmem((count, cols, rows), f32),
            vmem((count, cols, rows), f32),
            vmem((count, 8, mine * count), jnp.int32),
            vmem((cols, order), f32),
            vmem((cols, order), f32),
            vmem((cols, order), f32),
            vmem((2 * cols, order), half),
            vmem((1, order), f32),
            vmem((order, 1), f32),
            vmem((2, 2 * rows), f32),
            vmem((cols, order), f32),
            vmem((cols, order), f32),
            vmem((2, cols, order), f32),
            vmem((count, cols, rows), f32),
            vmem((count, cols, rows), f32),
            vmem((cols, mine * count), f32),
            vmem((count, cols, mine * count), f32),
            vmem((mine * count, total), f32),
            dma((3, chips, chips)),
            dma((count, chips)),
            dma((3, chips)),
            dma((count,)),
            dma((count,)),
            dma((count,)),
            dma((count,)),
            dma((count,)),
            dma((2, chips)),
            dma((2, chips)),
            dma((count,)),
            dma((count,)),
            dma((count,)),
            dma((count,)),
        ],
        compiler_params=pltpu.CompilerParams(
            collective_id=0, has_side_effects=True, vmem_limit_bytes=48 * 2**20
        ),
        cost_estimate=pl.CostEstimate(
            flops=36 * order * order * cols, bytes_accessed=16 * rows * order, transcendentals=0
        ),
    )(diag_blocks[0], coupling[0], sources[0], spots)
    return panels[None], picked[None]


def solution(mesh):
    placed = (
        P("depth", "panel", None),
        P("depth", "panel", None),
        P("depth", "panel", None),
        P("depth", "panel"),
    )
    return jax.shard_map(
        per_device,
        mesh=mesh,
        in_specs=placed,
        out_specs=(P("depth", "panel", None), P("depth", "panel", None)),
        check_vma=False,
    )
```

```python
import jax
import jax.numpy as jnp
from jax import lax
from jax.experimental import pallas as pl
from jax.experimental.pallas import tpu as pltpu
from jax.sharding import PartitionSpec as P

ITERS = 2


highest = lax.Precision.HIGHEST


def passed_along(block, axis, distance):
    devices = range(lax.axis_size(axis))
    route = [(i - distance, i) for i in devices if i - distance in devices]
    return lax.ppermute(block, axis, route)


def product_rows(matrix, panel_rows):
    initial = jnp.zeros((matrix.shape[0], panel_rows.shape[1]), jnp.float32)
    shard_rows = lax.all_gather(panel_rows, "panel", axis=0, tiled=True)
    columns = lax.slice_in_dim(matrix, 0, shard_rows.shape[0], axis=1)
    return initial + jnp.dot(
        columns, shard_rows, precision=highest, preferred_element_type=jnp.float32
    )


def product_transposed(matrix, panel_rows):
    return lax.psum_scatter(
        lax.dot_general(
            matrix,
            panel_rows,
            (((0,), (0,)), ((), ())),
            precision=highest,
            preferred_element_type=jnp.float32,
        ),
        "panel",
        scatter_dimension=0,
        tiled=True,
    )


def jacobi(matrix, diag_part, right_hand):
    scaled = diag_part[:, None]
    iterate = right_hand / scaled
    for sweep_no in range(ITERS):
        image = product_rows(matrix, iterate)
        iterate = iterate + (right_hand - image) / scaled
    return iterate


def per_device_general(diag_blocks, coupling, sources, requests):
    depth_count = lax.axis_size("depth")
    depth_pos = lax.axis_index("depth")
    panel_pos = lax.axis_index("panel")
    block_count = diag_blocks.shape[0]
    row_count = diag_blocks.shape[1]
    local_cols = sources.shape[2]
    own_square = lax.dynamic_slice_in_dim(diag_blocks, panel_pos * row_count, row_count, 2)
    diag_part = jnp.diagonal(own_square, axis1=1, axis2=2)
    col_groups = max(1, local_cols // 128)
    col_width = local_cols // col_groups
    section_total = depth_count + col_groups - 1
    left_terms = jnp.zeros_like(sources)
    carried = jnp.zeros((row_count, col_width), jnp.float32)
    for section_no in range(section_total):
        column_pos = section_no - depth_pos
        active = (column_pos >= 0) & (column_pos < col_groups)
        col_start = jnp.clip(column_pos, 0, col_groups - 1) * col_width
        block_no = 0
        source_cols = lax.dynamic_slice_in_dim(sources[block_no], col_start, col_width, 1)
        stored = lax.dynamic_update_slice_in_dim(left_terms[block_no], carried, col_start, 1)
        left_terms = left_terms.at[block_no].set(jnp.where(active, stored, left_terms[block_no]))
        forward = jacobi(diag_blocks[block_no], diag_part[block_no], source_cols - carried)
        carried = product_transposed(coupling[block_no], forward)
        carried = passed_along(carried, "depth", 1)
    panels = jnp.zeros_like(sources)
    ahead = jnp.zeros((row_count, col_width), jnp.float32)
    for section_no in range(section_total):
        column_pos = section_no - (depth_count - 1 - depth_pos)
        active = (column_pos >= 0) & (column_pos < col_groups)
        col_start = jnp.clip(column_pos, 0, col_groups - 1) * col_width
        for block_no in reversed(range(block_count)):
            source_cols = lax.dynamic_slice_in_dim(sources[block_no], col_start, col_width, 1)
            left_cols = lax.dynamic_slice_in_dim(left_terms[block_no], col_start, col_width, 1)
            right_term = product_rows(coupling[block_no], ahead)
            ahead = jacobi(
                diag_blocks[block_no], diag_part[block_no], source_cols - left_cols - right_term
            )
            stored = lax.dynamic_update_slice_in_dim(panels[block_no], ahead, col_start, 1)
            panels = panels.at[block_no].set(jnp.where(active, stored, panels[block_no]))
        ahead = passed_along(ahead, "depth", -1)
    picked_rows = requests.shape[1]
    shard_rows = lax.all_gather(panels, "panel", axis=1, tiled=True)
    shard_len = shard_rows.shape[1]
    inside = (requests >= 0) & (requests < shard_len)
    clipped = jnp.clip(requests, 0, shard_len - 1)
    where_rows = jnp.broadcast_to(
        clipped[:, :, None], (block_count, picked_rows, shard_rows.shape[2])
    )
    taken = jnp.take_along_axis(shard_rows, where_rows, axis=1)
    picked = jnp.where(inside[:, :, None], taken, 0.0)
    return (panels, picked)


MESH = pl.DeviceIdType.MESH
LEFT, RIGHT, SIBLING = 0, 1, 2


def received(x, a, b, chips):
    if a == x or b == x:
        return False
    if a == b:
        return True
    if a > x and b > x:
        return a < b
    if a < x and b < x:
        return a > b
    return (a < x) == (x < chips // 2)


def split(value):
    high = value.astype(jnp.bfloat16)
    low = (value - high.astype(jnp.float32)).astype(jnp.bfloat16)
    return high, low


def sweep_kernel(
    diag_ref, coup_ref, src_ref, req_ref,
    out_ref, pick_ref,
    diag_all, coup_all, diag_hi, diag_lo, map_hi, map_lo, edge_hi, edge_lo, part_hi, part_lo, edge,
    src_out, src_in, req_in, rhs, iterate, forward, stacked, total, src_own, scale, scale_col, factors,
    left_in, ahead_in, link_out, res_out, res_in, pick_out, pick_in, pick_rows,
    load, d_send, d_recv, c_send, c_recv, s_send, s_recv, q_send, q_recv,
    chain_send, chain_recv, r_send, r_recv, p_send, p_recv,
):
    depth_count = lax.axis_size("depth")
    count = lax.axis_size("panel")
    depth = lax.axis_index("depth")
    me = lax.axis_index("panel")
    chips = count // 2
    chip = me // 2
    core = lax.rem(me, 2)
    rows = diag_ref.shape[0]
    order = diag_ref.shape[1]
    cols = src_out.shape[1]
    width = order // chips
    last = depth_count - 1

    loads = [
        pltpu.make_async_copy(src_ref, src_own, load.at[0]),
        pltpu.make_async_copy(diag_ref, diag_all.at[me], load.at[1]),
        pltpu.make_async_copy(coup_ref, coup_all.at[me], load.at[2]),
    ]
    for copy in loads:
        copy.start()
    barrier = pltpu.get_barrier_semaphore()
    for off in range(1, count):
        pl.semaphore_signal(
            barrier, inc=1, device_id={"panel": lax.rem(me + off, count)}, device_id_type=MESH
        )

    @pl.when(depth > 0)
    def _():
        pl.semaphore_signal(barrier, inc=1, device_id={"depth": depth - 1}, device_id_type=MESH)

    @pl.when(depth < last)
    def _():
        pl.semaphore_signal(barrier, inc=1, device_id={"depth": depth + 1}, device_id_type=MESH)

    loads[0].wait()
    src_out[...] = src_own[...].T.reshape(count, cols, rows)
    loads[1].wait()
    loads[2].wait()

    ends = (depth == 0).astype(jnp.int32) + (depth == last).astype(jnp.int32)
    pl.semaphore_wait(barrier, count + 1 - ends)

    neighbour = {LEFT: me - 2, RIGHT: me + 2, SIBLING: me + 1 - 2 * core}

    def diag_copy(way, a, b, of_core):
        slab = 2 * a + of_core
        part = diag_all.at[slab, :, pl.ds(b * width, width)]
        return pltpu.make_async_remote_copy(
            src_ref=part, dst_ref=part,
            send_sem=d_send.at[way, a, b], recv_sem=d_recv.at[slab, b],
            device_id={"panel": neighbour[way]}, device_id_type=MESH,
        )

    def coup_copy(way, a, of_core):
        slab = 2 * a + of_core
        part = coup_all.at[slab]
        return pltpu.make_async_remote_copy(
            src_ref=part, dst_ref=part,
            send_sem=c_send.at[way, a], recv_sem=c_recv.at[slab],
            device_id={"panel": neighbour[way]}, device_id_type=MESH,
        )

    def diag_ways(x, a, b):
        ways = []
        if a >= x and any(received(y, a, b, chips) for y in range(x)):
            ways.append(LEFT)
        if a <= x and any(received(y, a, b, chips) for y in range(x + 1, chips)):
            ways.append(RIGHT)
        if a == x or received(x, a, b, chips):
            ways.append(SIBLING)
        return ways

    def arrivals(x):
        for dist in range(1, chips):
            for a in (x - dist, x + dist):
                if 0 <= a < chips:
                    yield a

    def own_first(x, a):
        return sorted(range(chips), key=lambda b: abs(b - a))

    def src_copy(off):
        to = lax.rem(me + off, count)
        return pltpu.make_async_remote_copy(
            src_ref=src_out.at[to], dst_ref=src_in.at[me],
            send_sem=s_send.at[off], recv_sem=s_recv.at[off],
            device_id={"panel": to}, device_id_type=MESH,
        )

    def req_copy(off):
        return pltpu.make_async_remote_copy(
            src_ref=req_ref, dst_ref=req_in.at[me],
            send_sem=q_send.at[off], recv_sem=q_recv.at[off],
            device_id={"panel": lax.rem(me + off, count)}, device_id_type=MESH,
        )

    for off in range(1, count):
        src_copy(off).start()
        req_copy(off).start()
    src_in[me] = src_out[me]
    req_in[me] = req_ref[...]

    def coup_each(a, act):
        @pl.when((a >= chip) & (chip > 0))
        def _():
            act(coup_copy(LEFT, a, core))

        @pl.when((a <= chip) & (chip < chips - 1))
        def _():
            act(coup_copy(RIGHT, a, core))

        act(coup_copy(SIBLING, a, core))

    def coup_first():
        @pl.when(depth < last)
        def _():
            coup_each(chip, lambda copy: copy.start())

    for x in range(chips):
        @pl.when(chip == x)
        def _():
            for b in own_first(x, x):
                for way in diag_ways(x, x, b):
                    diag_copy(way, x, b, core).start()
            for a in arrivals(x):
                for b in own_first(x, a):
                    if received(x, a, b, chips):
                        diag_copy(SIBLING, a, b, core).wait_recv()
                        for way in diag_ways(x, a, b):
                            diag_copy(way, a, b, core).start()
                if x in (0, chips - 1) and abs(a - x) == 1:
                    for b in range(chips):
                        for way in diag_ways(x, x, b):
                            diag_copy(way, x, b, core).wait_send()
                    coup_first()
            if x not in (0, chips - 1):
                coup_first()
            for a in range(chips):
                for b in range(chips):
                    if a == x or received(x, a, b, chips):
                        diag_copy(SIBLING, a, b, 1 - core).wait_recv()

    for off in range(1, count):
        src_copy(off).wait_recv()
        req_copy(off).wait_recv()

    def expand(at, carry):
        a, b = at // chips, lax.rem(at, chips)
        straddle = (a < chip) != (b < chip)
        from_left = chip < chips // 2
        both_right = (a > chip) & (b > chip)
        got = (a == chip) | (
            (b != chip)
            & (
                (a == b)
                | (both_right & (a < b))
                | ((a < chip) & (b < chip) & (a > b))
                | (straddle & ((a < chip) == from_left))
            )
        )
        rows_at = pl.ds(pl.multiple_of(a * width, width), width)
        cols_at = pl.ds(pl.multiple_of(b * width, width), width)

        @pl.when(got)
        def _():
            high, low = split(diag_all[pl.ds(2 * a, 2), :, cols_at].reshape(width, width))
            diag_hi[rows_at, cols_at] = high
            diag_lo[rows_at, cols_at] = low

        @pl.when(jnp.logical_not(got))
        def _():
            high, low = split(diag_all[pl.ds(2 * b, 2), :, rows_at].reshape(width, width).T)
            diag_hi[rows_at, cols_at] = high
            diag_lo[rows_at, cols_at] = low

        return carry

    lax.fori_loop(0, chips * chips, expand, 0)

    eye = lax.broadcasted_iota(jnp.int32, (rows, rows), 0) == lax.broadcasted_iota(
        jnp.int32, (rows, rows), 1
    )
    for p in range(count):
        lanes = slice(p * rows, (p + 1) * rows)
        scale[:, lanes] = jnp.sum(
            jnp.where(eye, diag_all[p, :, lanes], 0.0), axis=0, keepdims=True
        )
        scale_col[lanes, :] = jnp.sum(
            jnp.where(eye, diag_all[p, :, lanes], 0.0), axis=1, keepdims=True
        )
        rhs[:, lanes] = src_in[p]

    tile = width
    tall = 2 * width
    tiny = 1.0 / order

    def sums(n, carry):
        at = pl.ds(pl.multiple_of(n * tile, tile), tile)
        total = jnp.sum(jnp.abs(diag_hi[:, at].astype(jnp.float32)) * tiny, axis=0, keepdims=True)
        return jnp.maximum(carry, total / scale[:, at])

    largest = lax.fori_loop(0, chips, sums, jnp.zeros((1, tile), jnp.float32))
    largest = jnp.max(largest, axis=1, keepdims=True) * (1.02 * order)
    largest = jnp.maximum(largest, 1.0)
    least = jnp.min(scale[...], axis=1, keepdims=True)
    factors[0:1] = jnp.broadcast_to(largest, (1, tile))
    factors[1:2] = jnp.broadcast_to(least, (1, tile))

    def identity(i, n):
        down = lax.broadcasted_iota(jnp.int32, (tile, tile), 0) + i * tile
        over = lax.broadcasted_iota(jnp.int32, (tile, tile), 1) + n * tile
        return down == over

    def over_diag(value, rows_at):
        part = scale_col[rows_at, :]
        ease = jnp.where(part > 1.0, 2.0**-30, 1.0)
        return (value * ease) * (1.0 / (part * ease))

    def across(at):
        return factors[1:2] / scale[:, at] / factors[0:1] / factors[0:1]

    def first_step(at_tile, carry):
        i, n = at_tile // chips, lax.rem(at_tile, chips)
        rows_at = pl.ds(pl.multiple_of(i * tile, tile), tile)
        at = pl.ds(pl.multiple_of(n * tile, tile), tile)
        ratio = diag_hi[rows_at, at].astype(jnp.float32) + diag_lo[rows_at, at].astype(jnp.float32)
        ratio = over_diag(ratio, rows_at)
        high, low = split((jnp.where(identity(i, n), 2.0, 0.0) - ratio) * across(at))
        edge_hi[rows_at, at] = high
        edge_lo[rows_at, at] = low
        return carry

    lax.fori_loop(0, chips * chips, first_step, 0)

    def dot(left, right, contract=0):
        return lax.dot_general(
            left, right, (((1,), (contract,)), ((), ())), preferred_element_type=jnp.float32
        )

    def second_step(at_tile, carry):
        i, n = at_tile // chips, lax.rem(at_tile, chips)
        rows_at = pl.ds(pl.multiple_of(i * tile, tile), tile)
        at = pl.ds(pl.multiple_of(n * tile, tile), tile)
        moved = dot(diag_hi[rows_at, :], edge_hi[:, at]) + (
            dot(diag_hi[rows_at, :], edge_lo[:, at]) + dot(diag_lo[rows_at, :], edge_hi[:, at])
        )
        start = edge_hi[rows_at, at].astype(jnp.float32) + edge_lo[rows_at, at].astype(jnp.float32)
        moved = jnp.where(identity(i, n), across(at), 0.0) - over_diag(moved, rows_at)
        high, low = split(start + moved)
        map_hi[rows_at, at] = high
        map_lo[rows_at, at] = low
        return carry

    def sides(dist):
        return [(chip - dist, chip - dist >= 0), (chip + dist, chip + dist < chips)]

    def pass_on(dist):
        for a, there in sides(dist):
            @pl.when(there)
            def _():
                coup_copy(SIBLING, a, core).wait_recv()
                coup_each(a, lambda copy: copy.start())

    at_end = (chip == 0) | (chip == chips - 1)
    sending = depth < last
    lax.fori_loop(0, chips * chips // 2, second_step, 0)

    @pl.when(sending & jnp.logical_not(at_end))
    def _():
        pass_on(1)

    lax.fori_loop(chips * chips // 2, chips * chips, second_step, 0)

    def add_slab(a, first, final=False):
        high, low = split(coup_all[pl.ds(2 * a, 2)].reshape(width, order))
        part_hi[...] = high
        part_lo[...] = low
        along = pl.ds(pl.multiple_of(a * width, width), width)

        def one(at_tile, carry):
            i, n = lax.rem(at_tile, order // tall), at_tile // (order // tall)
            rows_at = pl.ds(pl.multiple_of(i * tall, tall), tall)
            at = pl.ds(pl.multiple_of(n * tile, tile), tile)
            term = dot(map_hi[rows_at, along], part_hi[:, at]) + (
                dot(map_hi[rows_at, along], part_lo[:, at])
                + dot(map_lo[rows_at, along], part_hi[:, at])
            )
            term = term if first else edge[rows_at, at] + term
            if final:
                high, low = split(term)
                edge_hi[rows_at, at] = high
                edge_lo[rows_at, at] = low
            else:
                edge[rows_at, at] = term
            return carry

        lax.fori_loop(0, (order // tall) * chips, one, 0)

    @pl.when(sending)
    def _():
        coup_copy(SIBLING, chip, 1 - core).wait_recv()
        add_slab(chip, True)

    @pl.when(sending & jnp.logical_not(at_end))
    def _():
        for dist in range(1, chips - 1):
            if dist + 1 < chips - 1:
                pass_on(dist + 1)
            for a, there in sides(dist):
                @pl.when(there)
                def _():
                    coup_copy(SIBLING, a, 1 - core).wait_recv()
                    add_slab(a, False)

        def narrow(i, carry):
            rows_at = pl.ds(pl.multiple_of(i * tile, tile), tile)
            high, low = split(edge[rows_at, :])
            edge_hi[rows_at, :] = high
            edge_lo[rows_at, :] = low
            return carry

        lax.fori_loop(0, chips, narrow, 0)

    @pl.when(sending & at_end)
    def _():
        for dist in range(1, chips):
            pass_on(dist)
            a = jnp.where(chip == 0, dist, chip - dist)
            coup_copy(SIBLING, a, 1 - core).wait_recv()
            add_slab(a, False, dist == chips - 1)

    def product(part, high_ref, low_ref, contract, finish):
        for k in range(chips):
            lanes = slice(k * tile, (k + 1) * tile)
            high, low = split(part(k, lanes))
            stacked[0:cols] = high
            stacked[cols : 2 * cols] = low

            def term(at):
                pick = (lanes, at) if contract == 0 else (at, lanes)
                both = dot(stacked[...], high_ref[pick], contract)
                small = dot(stacked[0:cols], low_ref[pick], contract)
                return both[0:cols] + (both[cols : 2 * cols] + small)

            def add(n, carry):
                at = pl.ds(pl.multiple_of(n * tile, tile), tile)
                total[:, at] = term(at) if k == 0 else total[:, at] + term(at)
                return carry

            def end(n, carry):
                at = pl.ds(pl.multiple_of(n * tile, tile), tile)
                image = total[:, at] + term(at)
                finish(n, at, image * factors[0:1] / factors[1:2] * factors[0:1])
                return carry

            lax.fori_loop(0, chips, add if k < chips - 1 else end, 0, unroll=k < chips - 1)

    def chain_copy(way, n, to):
        at = pl.ds(pl.multiple_of(n * tile, tile), tile)
        into = left_in if way == 0 else ahead_in
        return pltpu.make_async_remote_copy(
            src_ref=link_out.at[way, :, at], dst_ref=into.at[:, at],
            send_sem=chain_send.at[way, n], recv_sem=chain_recv.at[way, n],
            device_id={"depth": to}, device_id_type=MESH,
        )

    def send_left(n, at, image):
        link_out[0, :, at] = image
        chain_copy(0, n, depth + 1).start()

    def keep_forward(n, at, image):
        forward[:, at] = image

    def send_panel(n, at, image):
        iterate[:, at] = image

        @pl.when(depth > 0)
        def _():
            link_out[1, :, at] = image
            chain_copy(1, n, depth - 1).start()

    def rest_part(k, lanes):
        @pl.when(depth > 0)
        def _():
            chain_copy(0, k, depth).wait_recv()
            rhs[:, lanes] = rhs[:, lanes] - left_in[:, lanes]

        return rhs[:, lanes]

    def ahead_part(k, lanes):
        chain_copy(1, k, depth).wait_recv()
        return ahead_in[:, lanes]

    @pl.when(depth < last)
    def _():
        product(rest_part, edge_hi, edge_lo, 0, send_left)
        product(lambda k, lanes: rhs[:, lanes], map_hi, map_lo, 0, keep_forward)
        product(
            ahead_part, edge_hi, edge_lo, 1,
            lambda n, at, image: send_panel(n, at, forward[:, at] - image),
        )

    @pl.when(depth == last)
    def _():
        product(rest_part, map_hi, map_lo, 0, send_panel)

    def res_copy(off):
        to = lax.rem(me + off, count)
        return pltpu.make_async_remote_copy(
            src_ref=res_out.at[to], dst_ref=res_in.at[me],
            send_sem=r_send.at[off], recv_sem=r_recv.at[off],
            device_id={"panel": to}, device_id_type=MESH,
        )

    def pick_copy(off):
        return pltpu.make_async_remote_copy(
            src_ref=pick_out, dst_ref=pick_in.at[me],
            send_sem=p_send.at[off], recv_sem=p_recv.at[off],
            device_id={"panel": lax.rem(me + off, count)}, device_id_type=MESH,
        )

    for p in range(count):
        res_out[p] = iterate[:, p * rows : (p + 1) * rows]
    for off in range(1, count):
        res_copy(off).start()
    value = iterate[...]
    high, low = split(value)
    rest = ((value - high.astype(jnp.float32)) - low.astype(jnp.float32)).astype(jnp.bfloat16)
    wanted = jnp.sum(req_in[...], axis=0)[0:1]
    chosen = lax.broadcasted_iota(jnp.int32, (order, wanted.shape[1]), 0) == wanted
    chosen = chosen.astype(jnp.float32).astype(jnp.bfloat16)

    def take(term):
        return jnp.dot(term, chosen, preferred_element_type=jnp.float32)

    pick_out[...] = (take(rest) + take(low)) + take(high)
    for off in range(1, count):
        pick_copy(off).start()
    res_in[me] = res_out[me]
    pick_in[me] = pick_out[...]
    for off in range(1, count):
        res_copy(off).wait_recv()
    out_ref[...] = res_in[...].reshape(count * cols, rows).T
    for off in range(1, count):
        pick_copy(off).wait_recv()
    pick_rows[...] = pick_in[...].reshape(count * cols, pick_out.shape[1]).T
    mine = pick_ref.shape[0]
    pick_ref[...] = pick_rows[pl.ds(pl.multiple_of(me * mine, mine), mine), :]

    for off in range(1, count):
        src_copy(off).wait_send()
        req_copy(off).wait_send()
        res_copy(off).wait_send()
        pick_copy(off).wait_send()

    @pl.when(depth < last)
    def _():
        for n in range(chips):
            chain_copy(0, n, depth + 1).wait_send()
        for a in range(chips):
            coup_each(a, lambda copy: copy.wait_send())

    @pl.when(depth > 0)
    def _():
        for n in range(chips):
            chain_copy(1, n, depth - 1).wait_send()

    for x in range(chips):
        @pl.when(chip == x)
        def _():
            for a in range(chips):
                for b in range(chips):
                    for way in diag_ways(x, a, b):
                        if x not in (0, chips - 1) or a != x:
                            diag_copy(way, a, b, core).wait_send()


def per_device(diag_blocks, coupling, sources, requests):
    count = lax.axis_size("panel")
    block_count, rows, order = diag_blocks.shape
    total = sources.shape[2]
    mine = requests.shape[1]
    if (
        block_count != 1
        or count % 2
        or count < 4
        or rows % 128
        or order != rows * count
        or total % (16 * count)
        or mine % 8
        or (mine * count) % 128
    ):
        return per_device_general(diag_blocks, coupling, sources, requests)
    cols = total // count
    chips = count // 2
    spots = jnp.zeros((1, mine * count), jnp.int32)
    spots = lax.dynamic_update_slice(spots, requests, (0, lax.axis_index("panel") * mine))
    spots = jnp.broadcast_to(spots, (8, mine * count))
    f32, half = jnp.float32, jnp.bfloat16
    vmem = pltpu.VMEM
    dma = pltpu.SemaphoreType.DMA
    panels, picked = pl.pallas_call(
        sweep_kernel,
        out_shape=(
            jax.ShapeDtypeStruct((rows, total), f32),
            jax.ShapeDtypeStruct((mine, total), f32),
        ),
        in_specs=[pl.BlockSpec(memory_space=pl.ANY)] * 3 + [pl.BlockSpec(memory_space=vmem)],
        out_specs=(pl.BlockSpec(memory_space=vmem), pl.BlockSpec(memory_space=vmem)),
        scratch_shapes=[
            vmem((count, rows, order), f32),
            vmem((count, rows, order), f32),
            vmem((order, order), half),
            vmem((order, order), half),
            vmem((order, order), half),
            vmem((order, order), half),
            vmem((order, order), half),
            vmem((order, order), half),
            vmem((2 * rows, order), half),
            vmem((2 * rows, order), half),
            vmem((order, order), f32),
            vmem((count, cols, rows), f32),
            vmem((count, cols, rows), f32),
            vmem((count, 8, mine * count), jnp.int32),
            vmem((cols, order), f32),
            vmem((cols, order), f32),
            vmem((cols, order), f32),
            vmem((2 * cols, 2 * rows), half),
            vmem((cols, order), f32),
            vmem((rows, total), f32),
            vmem((1, order), f32),
            vmem((order, 1), f32),
            vmem((2, 2 * rows), f32),
            vmem((cols, order), f32),
            vmem((cols, order), f32),
            vmem((2, cols, order), f32),
            vmem((count, cols, rows), f32),
            vmem((count, cols, rows), f32),
            vmem((cols, mine * count), f32),
            vmem((count, cols, mine * count), f32),
            vmem((mine * count, total), f32),
            dma((3,)),
            dma((3, chips, chips)),
            dma((count, chips)),
            dma((3, chips)),
            dma((count,)),
            dma((count,)),
            dma((count,)),
            dma((count,)),
            dma((count,)),
            dma((2, chips)),
            dma((2, chips)),
            dma((count,)),
            dma((count,)),
            dma((count,)),
            dma((count,)),
        ],
        compiler_params=pltpu.CompilerParams(
            collective_id=0, has_side_effects=True, vmem_limit_bytes=48 * 2**20
        ),
        cost_estimate=pl.CostEstimate(
            flops=36 * order * order * cols, bytes_accessed=16 * rows * order, transcendentals=0
        ),
    )(diag_blocks[0], coupling[0], sources[0], spots)
    return panels[None], picked[None]


def solution(mesh):
    placed = (
        P("depth", "panel", None),
        P("depth", "panel", None),
        P("depth", "panel", None),
        P("depth", "panel"),
    )
    return jax.shard_map(
        per_device,
        mesh=mesh,
        in_specs=placed,
        out_specs=(P("depth", "panel", None), P("depth", "panel", None)),
        check_vma=False,
    )
```

```python
import jax
import jax.numpy as jnp
from jax import lax
from jax.experimental import pallas as pl
from jax.experimental.pallas import tpu as pltpu
from jax.sharding import PartitionSpec as P

ITERS = 2


highest = lax.Precision.HIGHEST


def passed_along(block, axis, distance):
    devices = range(lax.axis_size(axis))
    route = [(i - distance, i) for i in devices if i - distance in devices]
    return lax.ppermute(block, axis, route)


def product_rows(matrix, panel_rows):
    initial = jnp.zeros((matrix.shape[0], panel_rows.shape[1]), jnp.float32)
    shard_rows = lax.all_gather(panel_rows, "panel", axis=0, tiled=True)
    columns = lax.slice_in_dim(matrix, 0, shard_rows.shape[0], axis=1)
    return initial + jnp.dot(
        columns, shard_rows, precision=highest, preferred_element_type=jnp.float32
    )


def product_transposed(matrix, panel_rows):
    return lax.psum_scatter(
        lax.dot_general(
            matrix,
            panel_rows,
            (((0,), (0,)), ((), ())),
            precision=highest,
            preferred_element_type=jnp.float32,
        ),
        "panel",
        scatter_dimension=0,
        tiled=True,
    )


def jacobi(matrix, diag_part, right_hand):
    scaled = diag_part[:, None]
    iterate = right_hand / scaled
    for sweep_no in range(ITERS):
        image = product_rows(matrix, iterate)
        iterate = iterate + (right_hand - image) / scaled
    return iterate


def per_device_general(diag_blocks, coupling, sources, requests):
    depth_count = lax.axis_size("depth")
    depth_pos = lax.axis_index("depth")
    panel_pos = lax.axis_index("panel")
    block_count = diag_blocks.shape[0]
    row_count = diag_blocks.shape[1]
    local_cols = sources.shape[2]
    own_square = lax.dynamic_slice_in_dim(diag_blocks, panel_pos * row_count, row_count, 2)
    diag_part = jnp.diagonal(own_square, axis1=1, axis2=2)
    col_groups = max(1, local_cols // 128)
    col_width = local_cols // col_groups
    section_total = depth_count + col_groups - 1
    left_terms = jnp.zeros_like(sources)
    carried = jnp.zeros((row_count, col_width), jnp.float32)
    for section_no in range(section_total):
        column_pos = section_no - depth_pos
        active = (column_pos >= 0) & (column_pos < col_groups)
        col_start = jnp.clip(column_pos, 0, col_groups - 1) * col_width
        block_no = 0
        source_cols = lax.dynamic_slice_in_dim(sources[block_no], col_start, col_width, 1)
        stored = lax.dynamic_update_slice_in_dim(left_terms[block_no], carried, col_start, 1)
        left_terms = left_terms.at[block_no].set(jnp.where(active, stored, left_terms[block_no]))
        forward = jacobi(diag_blocks[block_no], diag_part[block_no], source_cols - carried)
        carried = product_transposed(coupling[block_no], forward)
        carried = passed_along(carried, "depth", 1)
    panels = jnp.zeros_like(sources)
    ahead = jnp.zeros((row_count, col_width), jnp.float32)
    for section_no in range(section_total):
        column_pos = section_no - (depth_count - 1 - depth_pos)
        active = (column_pos >= 0) & (column_pos < col_groups)
        col_start = jnp.clip(column_pos, 0, col_groups - 1) * col_width
        for block_no in reversed(range(block_count)):
            source_cols = lax.dynamic_slice_in_dim(sources[block_no], col_start, col_width, 1)
            left_cols = lax.dynamic_slice_in_dim(left_terms[block_no], col_start, col_width, 1)
            right_term = product_rows(coupling[block_no], ahead)
            ahead = jacobi(
                diag_blocks[block_no], diag_part[block_no], source_cols - left_cols - right_term
            )
            stored = lax.dynamic_update_slice_in_dim(panels[block_no], ahead, col_start, 1)
            panels = panels.at[block_no].set(jnp.where(active, stored, panels[block_no]))
        ahead = passed_along(ahead, "depth", -1)
    picked_rows = requests.shape[1]
    shard_rows = lax.all_gather(panels, "panel", axis=1, tiled=True)
    shard_len = shard_rows.shape[1]
    inside = (requests >= 0) & (requests < shard_len)
    clipped = jnp.clip(requests, 0, shard_len - 1)
    where_rows = jnp.broadcast_to(
        clipped[:, :, None], (block_count, picked_rows, shard_rows.shape[2])
    )
    taken = jnp.take_along_axis(shard_rows, where_rows, axis=1)
    picked = jnp.where(inside[:, :, None], taken, 0.0)
    return (panels, picked)


MESH = pl.DeviceIdType.MESH
LEFT, RIGHT, SIBLING = 0, 1, 2


def received(x, a, b, chips):
    if a == x or b == x:
        return False
    if a == b:
        return True
    if a > x and b > x:
        return a < b
    if a < x and b < x:
        return a > b
    return (a < x) == (x < chips // 2)


def split(value):
    high = value.astype(jnp.bfloat16)
    low = (value - high.astype(jnp.float32)).astype(jnp.bfloat16)
    return high, low


def sweep_kernel(
    diag_ref, coup_ref, src_ref, req_ref,
    out_ref, pick_ref,
    diag_all, coup_all, diag_hi, diag_lo, map_hi, map_lo, edge_hi, edge_lo, part_hi, part_lo, edge,
    src_out, src_in, req_in, rhs, iterate, forward, stacked, total, src_own, scale, scale_col, factors,
    left_in, ahead_in, link_out, res_out, res_in, pick_out, pick_in, pick_rows,
    load, d_send, d_recv, c_send, c_recv, s_send, s_recv, q_send, q_recv,
    chain_send, chain_recv, r_send, r_recv, p_send, p_recv,
):
    depth_count = lax.axis_size("depth")
    count = lax.axis_size("panel")
    depth = lax.axis_index("depth")
    me = lax.axis_index("panel")
    chips = count // 2
    chip = me // 2
    core = lax.rem(me, 2)
    rows = diag_ref.shape[0]
    order = diag_ref.shape[1]
    cols = src_out.shape[1]
    width = order // chips
    last = depth_count - 1

    loads = [
        pltpu.make_async_copy(src_ref, src_own, load.at[0]),
        pltpu.make_async_copy(diag_ref, diag_all.at[me], load.at[1]),
        pltpu.make_async_copy(coup_ref, coup_all.at[me], load.at[2]),
    ]
    for copy in loads:
        copy.start()
    barrier = pltpu.get_barrier_semaphore()
    for off in range(1, count):
        pl.semaphore_signal(
            barrier, inc=1, device_id={"panel": lax.rem(me + off, count)}, device_id_type=MESH
        )

    @pl.when(depth > 0)
    def _():
        pl.semaphore_signal(barrier, inc=1, device_id={"depth": depth - 1}, device_id_type=MESH)

    @pl.when(depth < last)
    def _():
        pl.semaphore_signal(barrier, inc=1, device_id={"depth": depth + 1}, device_id_type=MESH)

    loads[0].wait()
    src_out[...] = src_own[...].T.reshape(count, cols, rows)
    loads[1].wait()
    loads[2].wait()

    ends = (depth == 0).astype(jnp.int32) + (depth == last).astype(jnp.int32)
    pl.semaphore_wait(barrier, count + 1 - ends)

    neighbour = {LEFT: me - 2, RIGHT: me + 2, SIBLING: me + 1 - 2 * core}

    def diag_copy(way, a, b, of_core):
        slab = 2 * a + of_core
        part = diag_all.at[slab, :, pl.ds(b * width, width)]
        return pltpu.make_async_remote_copy(
            src_ref=part, dst_ref=part,
            send_sem=d_send.at[way, a, b], recv_sem=d_recv.at[slab, b],
            device_id={"panel": neighbour[way]}, device_id_type=MESH,
        )

    def coup_copy(way, a, of_core):
        slab = 2 * a + of_core
        part = coup_all.at[slab]
        return pltpu.make_async_remote_copy(
            src_ref=part, dst_ref=part,
            send_sem=c_send.at[way, a], recv_sem=c_recv.at[slab],
            device_id={"panel": neighbour[way]}, device_id_type=MESH,
        )

    def diag_ways(x, a, b):
        ways = []
        if a >= x and any(received(y, a, b, chips) for y in range(x)):
            ways.append(LEFT)
        if a <= x and any(received(y, a, b, chips) for y in range(x + 1, chips)):
            ways.append(RIGHT)
        if a == x or received(x, a, b, chips):
            ways.append(SIBLING)
        return ways

    def arrivals(x):
        for dist in range(1, chips):
            for a in (x - dist, x + dist):
                if 0 <= a < chips:
                    yield a

    def own_first(x, a):
        return sorted(range(chips), key=lambda b: abs(b - a))

    def src_copy(off):
        to = lax.rem(me + off, count)
        return pltpu.make_async_remote_copy(
            src_ref=src_out.at[to], dst_ref=src_in.at[me],
            send_sem=s_send.at[off], recv_sem=s_recv.at[off],
            device_id={"panel": to}, device_id_type=MESH,
        )

    def req_copy(off):
        return pltpu.make_async_remote_copy(
            src_ref=req_ref, dst_ref=req_in.at[me],
            send_sem=q_send.at[off], recv_sem=q_recv.at[off],
            device_id={"panel": lax.rem(me + off, count)}, device_id_type=MESH,
        )

    for off in range(1, count):
        src_copy(off).start()
        req_copy(off).start()
    src_in[me] = src_out[me]
    req_in[me] = req_ref[...]

    def coup_each(a, act):
        @pl.when((a >= chip) & (chip > 0))
        def _():
            act(coup_copy(LEFT, a, core))

        @pl.when((a <= chip) & (chip < chips - 1))
        def _():
            act(coup_copy(RIGHT, a, core))

        act(coup_copy(SIBLING, a, core))

    def coup_first():
        @pl.when(depth < last)
        def _():
            coup_each(chip, lambda copy: copy.start())

    for x in range(chips):
        @pl.when(chip == x)
        def _():
            for b in own_first(x, x):
                for way in diag_ways(x, x, b):
                    diag_copy(way, x, b, core).start()
            for a in arrivals(x):
                for b in own_first(x, a):
                    if received(x, a, b, chips):
                        diag_copy(SIBLING, a, b, core).wait_recv()
                        for way in diag_ways(x, a, b):
                            diag_copy(way, a, b, core).start()
                if x in (0, chips - 1) and abs(a - x) == 1:
                    for b in range(chips):
                        for way in diag_ways(x, x, b):
                            diag_copy(way, x, b, core).wait_send()
                    coup_first()
            if x not in (0, chips - 1):
                coup_first()
            for a in range(chips):
                for b in range(chips):
                    if a == x or received(x, a, b, chips):
                        diag_copy(SIBLING, a, b, 1 - core).wait_recv()

    for off in range(1, count):
        src_copy(off).wait_recv()
        req_copy(off).wait_recv()

    def expand(at, carry):
        a, b = at // chips, lax.rem(at, chips)
        straddle = (a < chip) != (b < chip)
        from_left = chip < chips // 2
        both_right = (a > chip) & (b > chip)
        got = (a == chip) | (
            (b != chip)
            & (
                (a == b)
                | (both_right & (a < b))
                | ((a < chip) & (b < chip) & (a > b))
                | (straddle & ((a < chip) == from_left))
            )
        )
        rows_at = pl.ds(pl.multiple_of(a * width, width), width)
        cols_at = pl.ds(pl.multiple_of(b * width, width), width)

        @pl.when(got)
        def _():
            high, low = split(diag_all[pl.ds(2 * a, 2), :, cols_at].reshape(width, width))
            diag_hi[rows_at, cols_at] = high
            diag_lo[rows_at, cols_at] = low

        @pl.when(jnp.logical_not(got))
        def _():
            high, low = split(diag_all[pl.ds(2 * b, 2), :, rows_at].reshape(width, width).T)
            diag_hi[rows_at, cols_at] = high
            diag_lo[rows_at, cols_at] = low

        return carry

    lax.fori_loop(0, chips * chips, expand, 0)

    eye = lax.broadcasted_iota(jnp.int32, (rows, rows), 0) == lax.broadcasted_iota(
        jnp.int32, (rows, rows), 1
    )
    for p in range(count):
        lanes = slice(p * rows, (p + 1) * rows)
        scale[:, lanes] = jnp.sum(
            jnp.where(eye, diag_all[p, :, lanes], 0.0), axis=0, keepdims=True
        )
        scale_col[lanes, :] = jnp.sum(
            jnp.where(eye, diag_all[p, :, lanes], 0.0), axis=1, keepdims=True
        )
        rhs[:, lanes] = src_in[p]

    tile = width
    tall = 2 * width
    tiny = 1.0 / order

    def sums(n, carry):
        at = pl.ds(pl.multiple_of(n * tile, tile), tile)
        total = jnp.sum(jnp.abs(diag_hi[:, at].astype(jnp.float32)) * tiny, axis=0, keepdims=True)
        return jnp.maximum(carry, total / scale[:, at])

    largest = lax.fori_loop(0, chips, sums, jnp.zeros((1, tile), jnp.float32))
    largest = jnp.max(largest, axis=1, keepdims=True) * (1.02 * order)
    largest = jnp.maximum(largest, 1.0)
    least = jnp.min(scale[...], axis=1, keepdims=True)
    factors[0:1] = jnp.broadcast_to(largest, (1, tile))
    factors[1:2] = jnp.broadcast_to(least, (1, tile))

    def identity(i, n):
        down = lax.broadcasted_iota(jnp.int32, (tile, tile), 0) + i * tile
        over = lax.broadcasted_iota(jnp.int32, (tile, tile), 1) + n * tile
        return down == over

    def over_diag(value, rows_at):
        part = scale_col[rows_at, :]
        ease = jnp.where(part > 1.0, 2.0**-30, 1.0)
        return (value * ease) * (1.0 / (part * ease))

    def across(at):
        return factors[1:2] / scale[:, at] / factors[0:1] / factors[0:1]

    def first_step(at_tile, carry):
        i, n = at_tile // chips, lax.rem(at_tile, chips)
        rows_at = pl.ds(pl.multiple_of(i * tile, tile), tile)
        at = pl.ds(pl.multiple_of(n * tile, tile), tile)
        ratio = diag_hi[rows_at, at].astype(jnp.float32) + diag_lo[rows_at, at].astype(jnp.float32)
        ratio = over_diag(ratio, rows_at)
        high, low = split((jnp.where(identity(i, n), 2.0, 0.0) - ratio) * across(at))
        edge_hi[rows_at, at] = high
        edge_lo[rows_at, at] = low
        return carry

    lax.fori_loop(0, chips * chips, first_step, 0)

    def dot(left, right, contract=0):
        return lax.dot_general(
            left, right, (((1,), (contract,)), ((), ())), preferred_element_type=jnp.float32
        )

    def second_step(at_tile, carry):
        i, n = at_tile // chips, lax.rem(at_tile, chips)
        rows_at = pl.ds(pl.multiple_of(i * tile, tile), tile)
        at = pl.ds(pl.multiple_of(n * tile, tile), tile)
        moved = dot(diag_hi[rows_at, :], edge_hi[:, at]) + (
            dot(diag_hi[rows_at, :], edge_lo[:, at]) + dot(diag_lo[rows_at, :], edge_hi[:, at])
        )
        start = edge_hi[rows_at, at].astype(jnp.float32) + edge_lo[rows_at, at].astype(jnp.float32)
        moved = jnp.where(identity(i, n), across(at), 0.0) - over_diag(moved, rows_at)
        high, low = split(start + moved)
        map_hi[rows_at, at] = high
        map_lo[rows_at, at] = low
        return carry

    def sides(dist):
        return [(chip - dist, chip - dist >= 0), (chip + dist, chip + dist < chips)]

    def pass_on(dist):
        for a, there in sides(dist):
            @pl.when(there)
            def _():
                coup_copy(SIBLING, a, core).wait_recv()
                coup_each(a, lambda copy: copy.start())

    at_end = (chip == 0) | (chip == chips - 1)
    sending = depth < last
    lax.fori_loop(0, chips * chips // 2, second_step, 0)

    @pl.when(sending & jnp.logical_not(at_end))
    def _():
        pass_on(1)

    lax.fori_loop(chips * chips // 2, chips * chips, second_step, 0)

    def add_slab(a, first, final=False):
        high, low = split(coup_all[pl.ds(2 * a, 2)].reshape(width, order))
        part_hi[...] = high
        part_lo[...] = low
        along = pl.ds(pl.multiple_of(a * width, width), width)

        def one(at_tile, carry):
            i, n = lax.rem(at_tile, order // tall), at_tile // (order // tall)
            rows_at = pl.ds(pl.multiple_of(i * tall, tall), tall)
            at = pl.ds(pl.multiple_of(n * tile, tile), tile)
            term = dot(map_hi[rows_at, along], part_hi[:, at]) + (
                dot(map_hi[rows_at, along], part_lo[:, at])
                + dot(map_lo[rows_at, along], part_hi[:, at])
            )
            term = term if first else edge[rows_at, at] + term
            if final:
                high, low = split(term)
                edge_hi[rows_at, at] = high
                edge_lo[rows_at, at] = low
            else:
                edge[rows_at, at] = term
            return carry

        lax.fori_loop(0, (order // tall) * chips, one, 0)

    @pl.when(sending)
    def _():
        coup_copy(SIBLING, chip, 1 - core).wait_recv()
        add_slab(chip, True)

    @pl.when(sending & jnp.logical_not(at_end))
    def _():
        for dist in range(1, chips - 1):
            if dist + 1 < chips - 1:
                pass_on(dist + 1)
            for a, there in sides(dist):
                @pl.when(there)
                def _():
                    coup_copy(SIBLING, a, 1 - core).wait_recv()
                    add_slab(a, False)

        def narrow(i, carry):
            rows_at = pl.ds(pl.multiple_of(i * tile, tile), tile)
            high, low = split(edge[rows_at, :])
            edge_hi[rows_at, :] = high
            edge_lo[rows_at, :] = low
            return carry

        lax.fori_loop(0, chips, narrow, 0)

    @pl.when(sending & at_end)
    def _():
        for dist in range(1, chips):
            pass_on(dist)
            a = jnp.where(chip == 0, dist, chip - dist)
            coup_copy(SIBLING, a, 1 - core).wait_recv()
            add_slab(a, False, dist == chips - 1)

    def product(part, high_ref, low_ref, contract, finish):
        for k in range(chips):
            lanes = slice(k * tile, (k + 1) * tile)
            high, low = split(part(k, lanes))
            stacked[0:cols] = high
            stacked[cols : 2 * cols] = low

            def term(at):
                pick = (lanes, at) if contract == 0 else (at, lanes)
                both = dot(stacked[...], high_ref[pick], contract)
                small = dot(stacked[0:cols], low_ref[pick], contract)
                return both[0:cols] + (both[cols : 2 * cols] + small)

            def add(n, carry):
                at = pl.ds(pl.multiple_of(n * tile, tile), tile)
                total[:, at] = term(at) if k == 0 else total[:, at] + term(at)
                return carry

            def end(n, carry):
                at = pl.ds(pl.multiple_of(n * tile, tile), tile)
                image = total[:, at] + term(at)
                finish(n, at, image * factors[0:1] / factors[1:2] * factors[0:1])
                return carry

            lax.fori_loop(0, chips, add if k < chips - 1 else end, 0, unroll=k < chips - 1)

    def chain_copy(way, n, to):
        at = pl.ds(pl.multiple_of(n * tile, tile), tile)
        into = left_in if way == 0 else ahead_in
        return pltpu.make_async_remote_copy(
            src_ref=link_out.at[way, :, at], dst_ref=into.at[:, at],
            send_sem=chain_send.at[way, n], recv_sem=chain_recv.at[way, n],
            device_id={"depth": to}, device_id_type=MESH,
        )

    def send_left(n, at, image):
        link_out[0, :, at] = image
        chain_copy(0, n, depth + 1).start()

    def keep_forward(n, at, image):
        forward[:, at] = image

    def send_panel(n, at, image):
        iterate[:, at] = image

        @pl.when(depth > 0)
        def _():
            link_out[1, :, at] = image
            chain_copy(1, n, depth - 1).start()

    def rest_part(k, lanes):
        @pl.when(depth > 0)
        def _():
            chain_copy(0, k, depth).wait_recv()
            rhs[:, lanes] = rhs[:, lanes] - left_in[:, lanes]

        return rhs[:, lanes]

    def ahead_part(k, lanes):
        chain_copy(1, k, depth).wait_recv()
        return ahead_in[:, lanes]

    @pl.when(depth < last)
    def _():
        product(rest_part, edge_hi, edge_lo, 0, send_left)
        product(lambda k, lanes: rhs[:, lanes], map_hi, map_lo, 0, keep_forward)
        product(
            ahead_part, edge_hi, edge_lo, 1,
            lambda n, at, image: send_panel(n, at, forward[:, at] - image),
        )

    @pl.when(depth == last)
    def _():
        product(rest_part, map_hi, map_lo, 0, send_panel)

    def res_copy(off):
        to = lax.rem(me + off, count)
        return pltpu.make_async_remote_copy(
            src_ref=res_out.at[to], dst_ref=res_in.at[me],
            send_sem=r_send.at[off], recv_sem=r_recv.at[off],
            device_id={"panel": to}, device_id_type=MESH,
        )

    def pick_copy(off):
        return pltpu.make_async_remote_copy(
            src_ref=pick_out, dst_ref=pick_in.at[me],
            send_sem=p_send.at[off], recv_sem=p_recv.at[off],
            device_id={"panel": lax.rem(me + off, count)}, device_id_type=MESH,
        )

    for p in range(count):
        res_out[p] = iterate[:, p * rows : (p + 1) * rows]
    for off in range(1, count):
        res_copy(off).start()
    value = iterate[...]
    high, low = split(value)
    rest = ((value - high.astype(jnp.float32)) - low.astype(jnp.float32)).astype(jnp.bfloat16)
    wanted = jnp.sum(req_in[...], axis=0)[0:1]
    chosen = lax.broadcasted_iota(jnp.int32, (order, wanted.shape[1]), 0) == wanted
    chosen = chosen.astype(jnp.float32).astype(jnp.bfloat16)

    def take(term):
        return jnp.dot(term, chosen, preferred_element_type=jnp.float32)

    pick_out[...] = (take(rest) + take(low)) + take(high)
    for off in range(1, count):
        pick_copy(off).start()
    res_in[me] = res_out[me]
    pick_in[me] = pick_out[...]
    for off in range(1, count):
        res_copy(off).wait_recv()
    out_ref[...] = res_in[...].reshape(count * cols, rows).T
    for off in range(1, count):
        pick_copy(off).wait_recv()
    pick_rows[...] = pick_in[...].reshape(count * cols, pick_out.shape[1]).T
    mine = pick_ref.shape[0]
    pick_ref[...] = pick_rows[pl.ds(pl.multiple_of(me * mine, mine), mine), :]

    for off in range(1, count):
        src_copy(off).wait_send()
        req_copy(off).wait_send()
        res_copy(off).wait_send()
        pick_copy(off).wait_send()

    @pl.when(depth < last)
    def _():
        for n in range(chips):
            chain_copy(0, n, depth + 1).wait_send()
        for a in range(chips):
            coup_each(a, lambda copy: copy.wait_send())

    @pl.when(depth > 0)
    def _():
        for n in range(chips):
            chain_copy(1, n, depth - 1).wait_send()

    for x in range(chips):
        @pl.when(chip == x)
        def _():
            for a in range(chips):
                for b in range(chips):
                    for way in diag_ways(x, a, b):
                        if x not in (0, chips - 1) or a != x:
                            diag_copy(way, a, b, core).wait_send()


def per_device(diag_blocks, coupling, sources, requests):
    count = lax.axis_size("panel")
    block_count, rows, order = diag_blocks.shape
    total = sources.shape[2]
    mine = requests.shape[1]
    if (
        block_count != 1
        or count % 2
        or count < 4
        or rows % 128
        or order != rows * count
        or total % (16 * count)
        or mine % 8
        or (mine * count) % 128
    ):
        return per_device_general(diag_blocks, coupling, sources, requests)
    cols = total // count
    chips = count // 2
    spots = jnp.zeros((1, mine * count), jnp.int32)
    spots = lax.dynamic_update_slice(spots, requests, (0, lax.axis_index("panel") * mine))
    spots = jnp.broadcast_to(spots, (8, mine * count))
    f32, half = jnp.float32, jnp.bfloat16
    vmem = pltpu.VMEM
    dma = pltpu.SemaphoreType.DMA
    panels, picked = pl.pallas_call(
        sweep_kernel,
        out_shape=(
            jax.ShapeDtypeStruct((rows, total), f32),
            jax.ShapeDtypeStruct((mine, total), f32),
        ),
        in_specs=[pl.BlockSpec(memory_space=pltpu.HBM)] * 3 + [pl.BlockSpec(memory_space=vmem)],
        out_specs=(pl.BlockSpec(memory_space=vmem), pl.BlockSpec(memory_space=vmem)),
        scratch_shapes=[
            vmem((count, rows, order), f32),
            vmem((count, rows, order), f32),
            vmem((order, order), half),
            vmem((order, order), half),
            vmem((order, order), half),
            vmem((order, order), half),
            vmem((order, order), half),
            vmem((order, order), half),
            vmem((2 * rows, order), half),
            vmem((2 * rows, order), half),
            vmem((order, order), f32),
            vmem((count, cols, rows), f32),
            vmem((count, cols, rows), f32),
            vmem((count, 8, mine * count), jnp.int32),
            vmem((cols, order), f32),
            vmem((cols, order), f32),
            vmem((cols, order), f32),
            vmem((2 * cols, 2 * rows), half),
            vmem((cols, order), f32),
            vmem((rows, total), f32),
            vmem((1, order), f32),
            vmem((order, 1), f32),
            vmem((2, 2 * rows), f32),
            vmem((cols, order), f32),
            vmem((cols, order), f32),
            vmem((2, cols, order), f32),
            vmem((count, cols, rows), f32),
            vmem((count, cols, rows), f32),
            vmem((cols, mine * count), f32),
            vmem((count, cols, mine * count), f32),
            vmem((mine * count, total), f32),
            dma((3,)),
            dma((3, chips, chips)),
            dma((count, chips)),
            dma((3, chips)),
            dma((count,)),
            dma((count,)),
            dma((count,)),
            dma((count,)),
            dma((count,)),
            dma((2, chips)),
            dma((2, chips)),
            dma((count,)),
            dma((count,)),
            dma((count,)),
            dma((count,)),
        ],
        compiler_params=pltpu.CompilerParams(
            collective_id=0, has_side_effects=True, vmem_limit_bytes=62 * 2**20
        ),
        cost_estimate=pl.CostEstimate(
            flops=36 * order * order * cols, bytes_accessed=16 * rows * order, transcendentals=0
        ),
    )(diag_blocks[0], coupling[0], sources[0], spots)
    return panels[None], picked[None]


def solution(mesh):
    placed = (
        P("depth", "panel", None),
        P("depth", "panel", None),
        P("depth", "panel", None),
        P("depth", "panel"),
    )
    return jax.shard_map(
        per_device,
        mesh=mesh,
        in_specs=placed,
        out_specs=(P("depth", "panel", None), P("depth", "panel", None)),
        check_vma=False,
    )
```
